256 devices in a mesh: replica: 32 (over z, x), tensor: 8 (over y, core).
Axes of the slice: x: 4, y: 4, z: 8, core: 2. Of those that a mesh axis runs over, the one named last changes fastest.
Arguments:
- momentum: float32 [32, 256, 27648], P('replica', None, 'tensor'), may hold values from -6 to 6
- grads: bfloat16 [32, 2, 256, 27648], P('replica', None, None, 'tensor'), may hold values from -1500 to 1500, as said below
Outputs:
- new_momentum: float32 [32, 256, 27648], P('replica', None, 'tensor')
- update: bfloat16 [256, 27648], P(None, 'tensor')
The draws below stay inside these ranges and needn't reach their ends.
Inputs may be any that keep to these rules, and one draw needn't show every extreme that they name: `grads`: gradients of each replica and step; magnitudes vary over rows, hidden units, replicas and steps.
All inputs are finite; a program needn't handle non-finite values.
Results may differ from the reference program's by a relative error of at most 0.001.
Values sent between devices are 32-bit elements; how exact they have to be, the bound alone decides.
A program may use at most 128 MiB of HBM per device.

```python
import math
import jax
import jax.numpy as jnp
from jax import lax

FF = 27648
ROWS = 256
TILE = 32
BAND = 8
STEPS = 2
REPLICAS = 32


def draw_grads(key, part):
    key = jax.random.fold_in(key, 11)
    key_noise = jax.random.fold_in(key, 0)
    key_rows = jax.random.fold_in(key, 1)
    key_cols = jax.random.fold_in(key, 2)
    key_step = jax.random.fold_in(key, 4)
    shape = (REPLICAS, STEPS, ROWS, FF)
    row_scale = jnp.exp(jax.random.uniform(key_rows, (REPLICAS, STEPS, ROWS, 1), jnp.float32, 0.0, math.log(10.0)))
    col_pos = jnp.arange(FF, dtype=jnp.float32) / max(FF - 1, 1)
    col_scale = jnp.exp(jax.random.uniform(key_cols, (FF,), jnp.float32, 0.0, math.log(3.0))) * jnp.power(3.0, col_pos)
    rep_pos = jnp.arange(REPLICAS, dtype=jnp.float32) / max(REPLICAS - 1, 1)
    rep_scale = jnp.power(3.0, rep_pos).reshape(REPLICAS, 1, 1, 1)
    quiet_step = jax.random.randint(key_step, (), 0, STEPS)
    step_scale = jnp.where(jnp.arange(STEPS) == quiet_step, 0.01, 1.0).astype(jnp.float32).reshape(1, STEPS, 1, 1)
    base = jax.random.truncated_normal(key_noise, -5.0, 5.0, shape, jnp.float32)
    values = base * row_scale * col_scale.reshape(1, 1, 1, FF) * rep_scale * step_scale
    return values.astype(jnp.bfloat16)


def shard_levels(rng, shape, pieces, low, top_value):
    level = 1.0
    for dim, parts in pieces:
        heights = jax.random.uniform(jax.random.fold_in(jax.random.fold_in(rng, 6), dim), (parts,), jnp.float32, low / len(pieces), top_value / len(pieces))
        level = level * jnp.repeat(jnp.exp(heights), shape[dim] // parts).reshape((-1,) + (1,) * (len(shape) - 1 - dim))
    return level


def noise(key, extent, deviation, bound, shards=(), kind=jnp.bfloat16):
    result = jax.random.normal(key, extent, jnp.float32) * deviation
    if len(shards) > 0:
        result = shard_levels(key, extent, shards, -0.22, 0.18) * result
    return jnp.clip(result, min=-bound, max=bound).astype(kind)


def setup_inputs(seed: int = 0) -> dict:
    streams_of = jax.random.split(jax.random.key(seed), 3)
    return {
        "momentum": noise(streams_of[0], (REPLICAS, ROWS, FF), 1.0, 6.0, ((0, 32), (2, 8)), jnp.float32),
        "grads": draw_grads(jax.random.fold_in(streams_of[2], 71), 0),
    }


HIGH = lax.Precision.HIGHEST
BETA = 0.9
CLIP = 1.0
EPS = 1e-06

def band_matrix():
    freq = jnp.arange(BAND, dtype=jnp.float32)[:, None]
    place = jnp.arange(TILE, dtype=jnp.float32)[None, :]
    weight = jnp.where(freq == 0, math.sqrt(1.0 / TILE), math.sqrt(2.0 / TILE))
    return weight * jnp.cos(math.pi * (2.0 * place + 1.0) * freq / (2.0 * TILE))

def encode(field, low_band):
    row_count, col_count = field.shape
    tiles = field.reshape(row_count // TILE, TILE, col_count)
    half = jnp.einsum('kn,anf->akf', low_band, tiles, precision=HIGH)
    half = half.reshape(row_count // TILE, BAND, col_count // TILE, TILE)
    whole = jnp.einsum('ln,akfn->akfl', low_band, half, precision=HIGH)
    return whole.reshape(row_count // TILE * BAND, col_count // TILE * BAND)

def decode(band, low_band, row_count, col_count):
    blocks = band.reshape(row_count // TILE, BAND, col_count // TILE, BAND)
    half = jnp.einsum('ln,akfl->akfn', low_band, blocks, precision=HIGH)
    half = half.reshape(row_count // TILE, BAND, col_count)
    whole = jnp.einsum('kn,akf->anf', low_band, half, precision=HIGH)
    return whole.reshape(row_count, col_count)

def reference(momentum, grads):
    low_band = band_matrix()
    count = float(REPLICAS * ROWS * FF)
    state = momentum
    update_sum = jnp.zeros((ROWS, FF), jnp.float32)
    for step in range(STEPS):
        step_grads = grads[:, step]
        partial_sq = lax.map(lambda g: jnp.sum(jnp.square(g.astype(jnp.float32))), step_grads)
        total = jnp.sum(partial_sq)
        scale = jnp.minimum(1.0, CLIP / jnp.sqrt(total / count + EPS))

        def advance(pair):
            current, grad_piece = pair
            current = BETA * current + scale * grad_piece.astype(jnp.float32)
            band = encode(current, low_band)
            return (current - decode(band, low_band, ROWS, FF), band)
        state, bands = lax.map(advance, (state, step_grads))
        summed = lax.optimization_barrier(jnp.sum(bands, axis=0))
        update_sum = update_sum + decode(summed, low_band, ROWS, FF)
    return (state, update_sum.astype(jnp.bfloat16))
```

```python
import functools
import math

import jax
import jax.numpy as jnp
import ml_dtypes
import numpy as np
from jax import lax
from jax.experimental import pallas as pl
from jax.experimental.pallas import tpu as pltpu
from jax.sharding import PartitionSpec as P

TILE = 32
BAND = 8
STEPS = 2
BETA = 0.9
CLIP = 1.0
EPS = 1e-06

MESH = pl.DeviceIdType.MESH
F32 = jnp.float32
BF16 = jnp.bfloat16

REP = 32
TEN = 8
ROWS = 256
COLS = 3456
GCOL = 512
GROUPS = 7
LAST = COLS - (GROUPS - 1) * GCOL
BROW = ROWS // TILE * BAND
BCOL = GCOL // TILE * BAND
QUART = 16
PIECES = GROUPS * (BROW // QUART)


def tables():
    freq = np.arange(BAND, dtype=np.float64)[:, None]
    place = np.arange(TILE, dtype=np.float64)[None, :]
    weight = np.where(freq == 0, math.sqrt(1.0 / TILE), math.sqrt(2.0 / TILE))
    low = weight * np.cos(math.pi * (2.0 * place + 1.0) * freq / (2.0 * TILE))

    def split(a):
        hi = a.astype(ml_dtypes.bfloat16)
        lo = (a - hi.astype(np.float64)).astype(ml_dtypes.bfloat16)
        return hi, lo

    col_hi, col_lo = split(np.kron(np.eye(GCOL // TILE), low))
    row_hi, row_lo = split(np.kron(np.eye(ROWS // TILE), low))
    w_enc = np.concatenate([col_hi.T, col_lo.T], axis=1)
    l_enc = np.concatenate([row_hi, row_lo], axis=0)
    w_dec = np.concatenate([col_hi, col_hi, col_lo], axis=0)
    l_dec = np.concatenate([row_hi.T, row_hi.T, row_lo.T], axis=1)
    return w_enc, l_enc, w_dec, l_dec


def halves(a):
    hi = a.astype(BF16)
    return hi, (a - hi.astype(F32)).astype(BF16)


def dot(a, b):
    return jnp.dot(a, b, preferred_element_type=F32)


def decode_group(band, w_dec, l_dec):
    hi, lo = halves(band)
    wide = dot(jnp.concatenate([hi, lo, hi], axis=1), w_dec)
    hi, lo = halves(wide)
    return dot(l_dec, jnp.concatenate([hi, lo, hi], axis=0))


def sync_kernel(
    m_hbm, g_hbm, wenc_hbm, lenc_hbm, wdec_hbm, ldec_hbm,
    nm, summed, wdec, ldec,
    m_v, g_v, wenc, lenc, enc, band, band2, sq1, sq2, rbuf, abuf, scales,
    g_sem, m_sem, c_sem, s1_send, s1_recv, s2_send, s2_recv, r_send, r_recv, a_send, a_recv,
):
    rep = lax.axis_index("replica")
    ten = lax.axis_index("tensor")

    barrier = pltpu.get_barrier_semaphore()

    def greet_tensor(d, _):
        pl.semaphore_signal(barrier, inc=1, device_id={"tensor": lax.rem(ten + d, TEN)}, device_id_type=MESH)
        return 0

    def greet_replica(d, _):
        pl.semaphore_signal(barrier, inc=1, device_id={"replica": lax.rem(rep + d, REP)}, device_id_type=MESH)
        return 0

    def grad_copy(g, width):
        return pltpu.make_async_copy(
            g_hbm.at[0, :, :, pl.ds(g * GCOL, width)], g_v.at[g, :, :, pl.ds(0, width)], g_sem.at[g]
        )

    def mom_copy(g, width):
        return pltpu.make_async_copy(
            m_hbm.at[0, :, pl.ds(g * GCOL, width)], m_v.at[g, :, pl.ds(0, width)], m_sem.at[g]
        )

    widths = [GCOL] * (GROUPS - 1) + [LAST]
    for g in range(GROUPS):
        grad_copy(g, widths[g]).start()
    consts = [
        pltpu.make_async_copy(src, dst, c_sem.at[i])
        for i, (src, dst) in enumerate(((wenc_hbm, wenc), (lenc_hbm, lenc), (wdec_hbm, wdec), (ldec_hbm, ldec)))
    ]
    for copy in consts:
        copy.start()
    for g in range(GROUPS):
        mom_copy(g, widths[g]).start()

    lax.fori_loop(1, TEN, greet_tensor, 0)
    lax.fori_loop(1, REP, greet_replica, 0)

    m_v[GROUPS - 1, :, LAST:] = jnp.zeros((ROWS, GCOL - LAST), F32)
    g_v[GROUPS - 1, :, :, LAST:] = jnp.zeros((STEPS, ROWS, GCOL - LAST), BF16)

    def squares(g, sums):
        def rows(i, sums):
            at = pl.ds(pl.multiple_of(i * 16, 16), 16)
            x0 = g_v[g, 0, at, :].astype(F32)
            x1 = g_v[g, 1, at, :].astype(F32)
            return sums[0] + x0 * x0, sums[1] + x1 * x1

        return lax.fori_loop(0, ROWS // 16, rows, sums, unroll=4)

    sums = (jnp.zeros((16, GCOL), F32), jnp.zeros((16, GCOL), F32))

    def waited(g, sums):
        grad_copy(g, GCOL).wait()
        return squares(g, sums)

    sums = lax.fori_loop(0, GROUPS - 1, waited, sums)
    grad_copy(GROUPS - 1, LAST).wait()
    sums = squares(GROUPS - 1, sums)

    def lanes(x):
        x = jnp.sum(x, axis=0, keepdims=True)
        return x[:, :128] + x[:, 128:256] + x[:, 256:384] + x[:, 384:]

    sq1[ten] = jnp.concatenate([lanes(sums[0]), lanes(sums[1])], axis=0)
    pl.semaphore_wait(barrier, TEN - 1 + REP - 1)

    def send_tensor(d, _):
        pltpu.make_async_remote_copy(
            src_ref=sq1.at[ten], dst_ref=sq1.at[ten], send_sem=s1_send, recv_sem=s1_recv,
            device_id={"tensor": lax.rem(ten + d, TEN)}, device_id_type=MESH,
        ).start()
        return 0

    lax.fori_loop(1, TEN, send_tensor, 0)

    def drain(buf, count, send, recv):
        part = buf.at[pl.ds(0, count)]
        if send is not None:
            pltpu.make_async_copy(part, part, send).wait()
        if recv is not None:
            pltpu.make_async_copy(part, part, recv).wait()

    def encode_group(g):
        m_hi, m_lo = halves(m_v[g])
        w = wenc[...]
        part = dot(m_hi, w) + dot(m_lo, w)
        cols = [part]
        for s in range(STEPS):
            cols.append(dot(g_v[g, s], w))
        wide = jnp.concatenate([c[:, :BCOL] + c[:, BCOL:] for c in cols], axis=1)
        hi, lo = halves(wide)
        first = dot(lenc[...], hi)
        e = first[:BROW] + first[BROW:] + dot(lenc[:BROW], lo)
        for i in range(STEPS + 1):
            enc[g, i] = e[:, i * BCOL:(i + 1) * BCOL]

    def encode_waited(g, _):
        mom_copy(g, GCOL).wait()
        encode_group(g)
        return 0

    consts[0].wait()
    consts[1].wait()
    lax.fori_loop(0, 2, encode_waited, 0)

    drain(sq1, TEN - 1, s1_send, s1_recv)
    sq2[rep] = jnp.sum(sq1[...], axis=0)

    def send_replica(d, _):
        pltpu.make_async_remote_copy(
            src_ref=sq2.at[rep], dst_ref=sq2.at[rep], send_sem=s2_send, recv_sem=s2_recv,
            device_id={"replica": lax.rem(rep + d, REP)}, device_id_type=MESH,
        ).start()
        return 0

    lax.fori_loop(1, REP, send_replica, 0)

    lax.fori_loop(2, GROUPS - 1, encode_waited, 0)
    mom_copy(GROUPS - 1, LAST).wait()
    encode_group(GROUPS - 1)

    drain(sq2, REP - 1, s2_send, s2_recv)
    total = jnp.sum(jnp.sum(sq2[...], axis=0), axis=1, keepdims=True)
    total = jnp.broadcast_to(total, (STEPS, 128))
    count = float(REP * ROWS * TEN * COLS)
    scale = jnp.minimum(1.0, CLIP / jnp.sqrt(total / count + EPS))
    scales[...] = scale
    s0, s1 = scale[0:1], scale[1:2]

    for g in range(GROUPS):
        first = BETA * enc[g, 0] + s0 * enc[g, 1]
        second = s1 * enc[g, 2]
        band[pl.ds(4 * g, 4)] = (first + second).reshape(4, QUART, BCOL)
        band2[g] = BETA * first + second

    def send_piece(d, _):
        peer = lax.rem(rep + d, REP)

        @pl.when(peer < PIECES)
        def _():
            pltpu.make_async_remote_copy(
                src_ref=band.at[peer], dst_ref=rbuf.at[rep], send_sem=r_send, recv_sem=r_recv,
                device_id={"replica": peer}, device_id_type=MESH,
            ).start()

        return 0

    lax.fori_loop(1, REP, send_piece, 0)

    consts[2].wait()
    consts[3].wait()

    def momentum_group(g, _):
        sc = scales[...]
        t0, t1 = sc[0:1, 0:1], sc[1:2, 0:1]
        low = decode_group(band2[g], wdec[...], ldec[...])
        state = BETA * m_v[g] + t0 * g_v[g, 0].astype(F32)
        nm[g] = BETA * state + t1 * g_v[g, 1].astype(F32) - low
        return 0

    lax.fori_loop(0, 3, momentum_group, 0)

    owner = rep < PIECES

    @pl.when(owner)
    def _():
        rbuf[rep] = band[rep]
        drain(rbuf, REP - 1, None, r_recv)
        abuf[rep] = jnp.sum(rbuf[...], axis=0)

        def send_sum(d, _):
            pltpu.make_async_remote_copy(
                src_ref=abuf.at[rep], dst_ref=abuf.at[rep], send_sem=a_send, recv_sem=a_recv,
                device_id={"replica": lax.rem(rep + d, REP)}, device_id_type=MESH,
            ).start()
            return 0

        lax.fori_loop(1, REP, send_sum, 0)

    lax.fori_loop(3, GROUPS, momentum_group, 0)

    @pl.when(owner)
    def _():
        drain(rbuf, PIECES - 1, r_send, None)
        drain(rbuf, REP - 1, a_send, None)
        drain(abuf, PIECES - 1, None, a_recv)

    @pl.when(jnp.logical_not(owner))
    def _():
        drain(rbuf, PIECES, r_send, None)
        drain(abuf, PIECES, None, a_recv)

    summed[...] = abuf[...]


def write_kernel(nm, summed, wdec, ldec, out_m, out_u, upd, m_sem, u_sem):
    def m_copy(g, width):
        return pltpu.make_async_copy(nm.at[g, :, pl.ds(0, width)], out_m.at[0, :, pl.ds(g * GCOL, width)], m_sem.at[g])

    def u_copy(g, width):
        return pltpu.make_async_copy(upd.at[g, :, pl.ds(0, width)], out_u.at[:, pl.ds(g * GCOL, width)], u_sem.at[g])

    widths = [GCOL] * (GROUPS - 1) + [LAST]
    for g in range(GROUPS):
        m_copy(g, widths[g]).start()
    for g in range(GROUPS):
        piece = summed[pl.ds(4 * g, 4)].reshape(BROW, BCOL)
        upd[g] = decode_group(piece, wdec[...], ldec[...]).astype(BF16)
        u_copy(g, widths[g]).start()
    for g in range(GROUPS):
        m_copy(g, widths[g]).wait()
        u_copy(g, widths[g]).wait()


def per_device(momentum, grads):
    w_enc, l_enc, w_dec, l_dec = (jnp.asarray(t) for t in tables())
    hbm = pl.BlockSpec(memory_space=pl.ANY)
    vmem = pl.BlockSpec(memory_space=pltpu.VMEM)
    dma = pltpu.SemaphoreType.DMA
    nm, summed, wdec, ldec = pl.pallas_call(
        sync_kernel,
        out_shape=(
            pltpu.VMEM((GROUPS, ROWS, GCOL), F32),
            pltpu.VMEM((PIECES, QUART, BCOL), F32),
            pltpu.VMEM(w_dec.shape, BF16),
            pltpu.VMEM(l_dec.shape, BF16),
        ),
        in_specs=[hbm] * 6,
        out_specs=(vmem,) * 4,
        scratch_shapes=[
            pltpu.VMEM((GROUPS, ROWS, GCOL), F32),
            pltpu.VMEM((GROUPS, STEPS, ROWS, GCOL), BF16),
            pltpu.VMEM(w_enc.shape, BF16),
            pltpu.VMEM(l_enc.shape, BF16),
            pltpu.VMEM((GROUPS, STEPS + 1, BROW, BCOL), F32),
            pltpu.VMEM((PIECES, QUART, BCOL), F32),
            pltpu.VMEM((GROUPS, BROW, BCOL), F32),
            pltpu.VMEM((TEN, STEPS, 128), F32),
            pltpu.VMEM((REP, STEPS, 128), F32),
            pltpu.VMEM((REP, QUART, BCOL), F32),
            pltpu.VMEM((PIECES, QUART, BCOL), F32),
            pltpu.VMEM((STEPS, 128), F32),
            dma((GROUPS,)), dma((GROUPS,)), dma((4,)),
            dma, dma, dma, dma, dma, dma, dma, dma,
        ],
        compiler_params=pltpu.CompilerParams(
            collective_id=0, has_side_effects=True, vmem_limit_bytes=36 * 1024 * 1024
        ),
        name="sync",
    )(momentum, grads, w_enc, l_enc, w_dec, l_dec)
    return pl.pallas_call(
        write_kernel,
        out_shape=(
            jax.ShapeDtypeStruct((1, ROWS, COLS), F32),
            jax.ShapeDtypeStruct((ROWS, COLS), BF16),
        ),
        in_specs=[vmem] * 4,
        out_specs=(hbm, hbm),
        scratch_shapes=[pltpu.VMEM((GROUPS, ROWS, GCOL), BF16), dma((GROUPS,)), dma((GROUPS,))],
        compiler_params=pltpu.CompilerParams(vmem_limit_bytes=16 * 1024 * 1024),
        name="write",
    )(*(pltpu.with_memory_space_constraint(a, pltpu.VMEM) for a in (nm, summed, wdec, ldec)))


def solution(mesh):
    in_specs = (P("replica", None, "tensor"), P("replica", None, None, "tensor"))
    out_specs = (P("replica", None, "tensor"), P(None, "tensor"))
    return jax.shard_map(
        per_device, mesh=mesh, in_specs=in_specs, out_specs=out_specs, check_vma=False
    )
```

```python
import functools
import math

import jax
import jax.numpy as jnp
import ml_dtypes
import numpy as np
from jax import lax
from jax.experimental import pallas as pl
from jax.experimental.pallas import tpu as pltpu
from jax.sharding import PartitionSpec as P

TILE = 32
BAND = 8
STEPS = 2
BETA = 0.9
CLIP = 1.0
EPS = 1e-06

MESH = pl.DeviceIdType.MESH
F32 = jnp.float32
BF16 = jnp.bfloat16

REP = 32
TEN = 8
NX, NY, NZ, NC = 4, 4, 8, 2
PLANE = NX * NY * NC
ROWS = 256
COLS = 3456
GCOL = 512
GROUPS = 7
LAST = COLS - (GROUPS - 1) * GCOL
BROW = ROWS // TILE * BAND
BCOL = GCOL // TILE * BAND
QUART = 16
PIECES = GROUPS * (BROW // QUART)


def patterns():
    freq = np.arange(BAND, dtype=np.float64)[:, None]
    place = np.arange(TILE, dtype=np.float64)[None, :]
    weight = np.where(freq == 0, math.sqrt(1.0 / TILE), math.sqrt(2.0 / TILE))
    low = weight * np.cos(math.pi * (2.0 * place + 1.0) * freq / (2.0 * TILE))
    down = np.tile(low.T, (1, GCOL // BAND))
    across = np.tile(low, (1, GCOL // TILE))
    return np.concatenate([down, across], axis=0).astype(np.float32)


def block_diagonal(pattern, times, rows_per, cols_per):
    whole = jnp.concatenate([pattern] * times, axis=0)
    i = lax.broadcasted_iota(jnp.int32, whole.shape, 0) // rows_per
    j = lax.broadcasted_iota(jnp.int32, whole.shape, 1) // cols_per
    return halves(jnp.where(i == j, whole, 0.0))


def build_tables(pat, wenc, lenc, wdec, ldec):
    down, across = pat[:TILE], pat[TILE:]
    hi, lo = block_diagonal(down[:, :BCOL], GCOL // TILE, TILE, BAND)
    wenc[:, :BCOL] = hi
    wenc[:, BCOL:] = lo
    hi, lo = block_diagonal(across[:, :ROWS], ROWS // TILE, BAND, TILE)
    lenc[:BROW] = hi
    lenc[BROW:] = lo
    hi, lo = block_diagonal(across, GCOL // TILE, BAND, TILE)
    wdec[:BCOL] = hi
    wdec[BCOL:2 * BCOL] = hi
    wdec[2 * BCOL:] = lo
    hi, lo = block_diagonal(down[:, :BROW], ROWS // TILE, TILE, BAND)
    ldec[...] = jnp.concatenate([hi, hi, lo], axis=1)


def halves(a):
    hi = a.astype(BF16)
    return hi, (a - hi.astype(F32)).astype(BF16)


def dot(a, b):
    return jnp.dot(a, b, preferred_element_type=F32)


def decode_group(band, w_dec, l_dec):
    hi, lo = halves(band)
    wide = dot(jnp.concatenate([hi, lo, hi], axis=1), w_dec)
    hi, lo = halves(wide)
    return dot(l_dec, jnp.concatenate([hi, lo, hi], axis=0))


def far(k, n):
    return n // 2 + lax.div(k + 1, 2) * (1 - 2 * lax.rem(k, 2))


def drain(buf, count, sem):
    part = buf.at[pl.ds(0, count)]
    pltpu.make_async_copy(part, part, sem).wait()


def sync_kernel(
    m_hbm, g_hbm, pat_hbm,
    nm, upd,
    m_v, g_v, pat, wenc, lenc, wdec, ldec, xs, xr, zs, zr, abuf, sq1, sq2, scales,
    g_sem, m_sem, c_sem, p1_send, p1_recv, p2_send, p2_recv, x_send, x_recv, z_send, z_recv, a_send, a_recv,
):
    rep = lax.axis_index("replica")
    ten = lax.axis_index("tensor")
    z, x = lax.div(rep, NX), lax.rem(rep, NX)
    y, c = lax.div(ten, NC), lax.rem(ten, NC)

    def plane_peer(k):
        dx, dy, dc = far(lax.div(k, NY * NC), NX), far(lax.rem(lax.div(k, NC), NY), NY), far(lax.rem(k, NC), NC)
        return {
            "replica": z * NX + lax.rem(x + dx, NX),
            "tensor": lax.rem(y + dy, NY) * NC + lax.rem(c + dc, NC),
        }

    def z_peer(d):
        return {"replica": lax.rem(z + d, NZ) * NX + x}

    def x_peer(d):
        return {"replica": z * NX + lax.rem(x + d, NX)}

    def replica_peer(k):
        dz, dx = far(lax.div(k, NX), NZ), far(lax.rem(k, NX), NX)
        return {"replica": lax.rem(z + dz, NZ) * NX + lax.rem(x + dx, NX)}

    def send(src, dst, send_sem, recv_sem, peer):
        pltpu.make_async_remote_copy(
            src_ref=src, dst_ref=dst, send_sem=send_sem, recv_sem=recv_sem, device_id=peer, device_id_type=MESH
        ).start()

    def grad_copy(g, width):
        return pltpu.make_async_copy(
            g_hbm.at[0, :, :, pl.ds(g * GCOL, width)], g_v.at[g, :, :, pl.ds(0, width)], g_sem.at[g]
        )

    def mom_copy(g, width):
        return pltpu.make_async_copy(
            m_hbm.at[0, :, pl.ds(g * GCOL, width)], m_v.at[g, :, pl.ds(0, width)], m_sem.at[g]
        )

    widths = [GCOL] * (GROUPS - 1) + [LAST]
    for g in range(GROUPS):
        grad_copy(g, widths[g]).start()

    barrier = pltpu.get_barrier_semaphore()

    def greet_z(k, _):
        pl.semaphore_signal(barrier, inc=1, device_id=z_peer(far(k, NZ)), device_id_type=MESH)
        return 0

    def greet_plane(k, _):
        pl.semaphore_signal(barrier, inc=1, device_id=plane_peer(k), device_id_type=MESH)
        return 0

    lax.fori_loop(0, NZ - 1, greet_z, 0)
    lax.fori_loop(0, PLANE - 1, greet_plane, 0)

    pattern = pltpu.make_async_copy(pat_hbm, pat, c_sem)
    pattern.start()
    for g in range(GROUPS):
        mom_copy(g, widths[g]).start()
    pattern.wait()
    build_tables(pat, wenc, lenc, wdec, ldec)

    m_v[GROUPS - 1, :, LAST:] = jnp.zeros((ROWS, GCOL - LAST), F32)
    g_v[GROUPS - 1, :, :, LAST:] = jnp.zeros((STEPS, ROWS, GCOL - LAST), BF16)

    def squares(g, sums):
        def rows(i, sums):
            at = pl.ds(pl.multiple_of(i * 16, 16), 16)
            x0 = g_v[g, 0, at, :].astype(F32)
            x1 = g_v[g, 1, at, :].astype(F32)
            return sums[0] + x0 * x0, sums[1] + x1 * x1

        return lax.fori_loop(0, ROWS // 16, rows, sums, unroll=4)

    def waited(g, sums):
        grad_copy(g, GCOL).wait()
        return squares(g, sums)

    sums = (jnp.zeros((16, GCOL), F32), jnp.zeros((16, GCOL), F32))
    sums = lax.fori_loop(0, GROUPS - 1, waited, sums)
    grad_copy(GROUPS - 1, LAST).wait()
    sums = squares(GROUPS - 1, sums)

    def lanes(v):
        v = jnp.sum(v, axis=0, keepdims=True)
        return v[:, :128] + v[:, 128:256] + v[:, 256:384] + v[:, 384:]

    here = (x * NY + y) * NC + c
    sq1[here] = jnp.concatenate([lanes(sums[0]), lanes(sums[1])], axis=0)
    pl.semaphore_wait(barrier, NZ - 1 + PLANE - 1)

    def send_plane(k, _):
        send(sq1.at[here], sq1.at[here], p1_send, p1_recv, plane_peer(k))
        return 0

    lax.fori_loop(0, PLANE - 1, send_plane, 0)

    def encode_group(g):
        m_hi, m_lo = halves(m_v[g])
        w = wenc[...]
        cols = [dot(m_hi, w) + dot(m_lo, w)]
        for s in range(STEPS):
            cols.append(dot(g_v[g, s], w))
        wide = jnp.concatenate([v[:, :BCOL] + v[:, BCOL:] for v in cols], axis=1)
        hi, lo = halves(wide)
        first = dot(lenc[...], hi)
        e = first[:BROW] + first[BROW:] + dot(lenc[:BROW], lo)
        for i in range(STEPS + 1):
            xs[:, g, i] = e[:, i * BCOL:(i + 1) * BCOL].reshape(NX, QUART, BCOL)

    def send_quarters(g):
        for d in (2, 1, 3):
            send(xs.at[lax.rem(x + d, NX), g], xr.at[d - 1, g], x_send, x_recv, x_peer(d))

    def encode_waited(g, _):
        mom_copy(g, GCOL).wait()
        encode_group(g)
        send_quarters(g)
        return 0

    lax.fori_loop(0, GROUPS - 1, encode_waited, 0)
    mom_copy(GROUPS - 1, LAST).wait()
    encode_group(GROUPS - 1)
    send_quarters(GROUPS - 1)

    drain(sq1, PLANE - 1, p1_recv)
    sq2[z] = jnp.sum(sq1[...], axis=0)

    def send_z(k, _):
        send(sq2.at[z], sq2.at[z], p2_send, p2_recv, z_peer(far(k, NZ)))
        return 0

    lax.fori_loop(0, NZ - 1, send_z, 0)

    drain(xr, NX - 1, x_recv)
    mine = xs[x] + xr[0] + xr[1] + xr[2]

    drain(sq2, NZ - 1, p2_recv)
    total = jnp.sum(jnp.sum(sq2[...], axis=0), axis=1, keepdims=True)
    total = jnp.broadcast_to(total, (STEPS, 128))
    count = float(REP * ROWS * TEN * COLS)
    scale = jnp.minimum(1.0, CLIP / jnp.sqrt(total / count + EPS))
    scales[...] = scale
    s0, s1 = scale[0:1], scale[1:2]
    zs[...] = BETA * mine[:, 0] + s0 * mine[:, 1] + s1 * mine[:, 2]

    def send_group(k, _):
        d = far(k, NZ)
        peer = lax.rem(z + d, NZ)

        @pl.when(peer < GROUPS)
        def _():
            send(zs.at[peer], zr.at[d - 1], z_send, z_recv, z_peer(d))

        return 0

    lax.fori_loop(0, NZ - 1, send_group, 0)

    def momentum_group(g, _):
        sc = scales[...]
        t0, t1 = sc[0:1], sc[1:2]
        own = BETA * (BETA * xs[:, g, 0] + t0 * xs[:, g, 1]) + t1 * xs[:, g, 2]
        low = decode_group(own.reshape(BROW, BCOL), wdec[...], ldec[...])
        state = BETA * m_v[g] + t0[:, 0:1] * g_v[g, 0].astype(F32)
        nm[g] = BETA * state + t1[:, 0:1] * g_v[g, 1].astype(F32) - low
        return 0

    lax.fori_loop(0, 3, momentum_group, 0)

    owner = z < GROUPS

    @pl.when(owner)
    def _():
        drain(zr, NZ - 1, z_recv)
        abuf[rep] = zs[z] + jnp.sum(zr[...], axis=0)

        def send_sum(k, _):
            send(abuf.at[rep], abuf.at[rep], a_send, a_recv.at[z], replica_peer(k))
            return 0

        lax.fori_loop(0, REP - 1, send_sum, 0)

    lax.fori_loop(3, GROUPS, momentum_group, 0)

    def decode_sum(k, _):
        g = lax.rem(z + NZ + lax.div(k + 1, 2) * (2 * lax.rem(k, 2) - 1), NZ)

        @pl.when(g < GROUPS)
        def _():
            @pl.when(g == z)
            def _():
                drain(abuf, NX - 1, a_recv.at[g])

            @pl.when(g != z)
            def _():
                drain(abuf, NX, a_recv.at[g])

            piece = abuf[pl.ds(NX * g, NX)].reshape(BROW, BCOL)
            upd[g] = decode_group(piece, wdec[...], ldec[...]).astype(BF16)

        return 0

    lax.fori_loop(0, NZ, decode_sum, 0)

    drain(sq1, PLANE - 1, p1_send)
    drain(sq2, NZ - 1, p2_send)
    drain(xr, NX - 1, x_send)

    @pl.when(owner)
    def _():
        drain(zs, GROUPS - 1, z_send)
        drain(abuf, PIECES, a_send)
        drain(abuf, REP - 1 - PIECES, a_send)

    @pl.when(jnp.logical_not(owner))
    def _():
        drain(zs, GROUPS, z_send)


def write_kernel(nm, upd, out_m, out_u, m_sem, u_sem):
    copies = []
    for g in range(GROUPS):
        width = GCOL if g < GROUPS - 1 else LAST
        here, there = pl.ds(0, width), pl.ds(g * GCOL, width)
        copies.append(pltpu.make_async_copy(nm.at[g, :, here], out_m.at[0, :, there], m_sem.at[g]))
        copies.append(pltpu.make_async_copy(upd.at[g, :, here], out_u.at[:, there], u_sem.at[g]))
    for copy in copies:
        copy.start()
    for copy in copies:
        copy.wait()


def per_device(momentum, grads):
    table = jnp.asarray(patterns())
    hbm = pl.BlockSpec(memory_space=pl.ANY)
    vmem = pl.BlockSpec(memory_space=pltpu.VMEM)
    dma = pltpu.SemaphoreType.DMA
    nm, upd = pl.pallas_call(
        sync_kernel,
        out_shape=(
            pltpu.VMEM((GROUPS, ROWS, GCOL), F32),
            pltpu.VMEM((GROUPS, ROWS, GCOL), BF16),
        ),
        in_specs=[hbm] * 3,
        out_specs=(vmem,) * 2,
        scratch_shapes=[
            pltpu.VMEM((GROUPS, ROWS, GCOL), F32),
            pltpu.VMEM((GROUPS, STEPS, ROWS, GCOL), BF16),
            pltpu.VMEM((TILE + BAND, GCOL), F32),
            pltpu.VMEM((GCOL, 2 * BCOL), BF16),
            pltpu.VMEM((2 * BROW, ROWS), BF16),
            pltpu.VMEM((3 * BCOL, GCOL), BF16),
            pltpu.VMEM((ROWS, 3 * BROW), BF16),
            pltpu.VMEM((NX, GROUPS, STEPS + 1, QUART, BCOL), F32),
            pltpu.VMEM((NX - 1, GROUPS, STEPS + 1, QUART, BCOL), F32),
            pltpu.VMEM((GROUPS, QUART, BCOL), F32),
            pltpu.VMEM((NZ - 1, QUART, BCOL), F32),
            pltpu.VMEM((PIECES, QUART, BCOL), F32),
            pltpu.VMEM((PLANE, STEPS, 128), F32),
            pltpu.VMEM((NZ, STEPS, 128), F32),
            pltpu.VMEM((STEPS, 128), F32),
            dma((GROUPS,)), dma((GROUPS,)), dma,
            dma, dma, dma, dma, dma, dma, dma, dma, dma, dma((GROUPS,)),
        ],
        compiler_params=pltpu.CompilerParams(
            collective_id=0, has_side_effects=True, vmem_limit_bytes=36 * 1024 * 1024
        ),
        name="sync",
    )(*(pltpu.with_memory_space_constraint(a, pltpu.HBM) for a in (momentum, grads, table)))
    return pl.pallas_call(
        write_kernel,
        out_shape=(
            jax.ShapeDtypeStruct((1, ROWS, COLS), F32),
            jax.ShapeDtypeStruct((ROWS, COLS), BF16),
        ),
        in_specs=[vmem] * 2,
        out_specs=(hbm, hbm),
        scratch_shapes=[dma((GROUPS,)), dma((GROUPS,))],
        compiler_params=pltpu.CompilerParams(vmem_limit_bytes=8 * 1024 * 1024),
        name="write",
    )(*(pltpu.with_memory_space_constraint(a, pltpu.VMEM) for a in (nm, upd)))


def solution(mesh):
    in_specs = (P("replica", None, "tensor"), P("replica", None, None, "tensor"))
    out_specs = (P("replica", None, "tensor"), P(None, "tensor"))
    return jax.shard_map(
        per_device, mesh=mesh, in_specs=in_specs, out_specs=out_specs, check_vma=False
    )
```

```python
import functools
import math

import jax
import jax.numpy as jnp
import ml_dtypes
import numpy as np
from jax import lax
from jax.experimental import pallas as pl
from jax.experimental.pallas import tpu as pltpu
from jax.sharding import PartitionSpec as P

TILE = 32
BAND = 8
STEPS = 2
BETA = 0.9
CLIP = 1.0
EPS = 1e-06

MESH = pl.DeviceIdType.MESH
F32 = jnp.float32
BF16 = jnp.bfloat16

REP = 32
TEN = 8
NX, NY, NZ, NC = 4, 4, 8, 2
PLANE = NX * NY * NC
IDLE = 4
ROWS = 256
COLS = 3456
GCOL = 512
GROUPS = 7
LAST = COLS - (GROUPS - 1) * GCOL
BROW = ROWS // TILE * BAND
BCOL = GCOL // TILE * BAND
QUART = 16
PIECES = GROUPS * (BROW // QUART)


def patterns():
    freq = np.arange(BAND, dtype=np.float64)[:, None]
    place = np.arange(TILE, dtype=np.float64)[None, :]
    weight = np.where(freq == 0, math.sqrt(1.0 / TILE), math.sqrt(2.0 / TILE))
    low = weight * np.cos(math.pi * (2.0 * place + 1.0) * freq / (2.0 * TILE))
    down = np.tile(low.T, (1, GCOL // BAND))
    across = np.tile(low, (1, GCOL // TILE))
    return np.concatenate([down, across], axis=0).astype(np.float32)


def block_diagonal(pattern, times, rows_per, cols_per):
    whole = jnp.concatenate([pattern] * times, axis=0)
    i = lax.broadcasted_iota(jnp.int32, whole.shape, 0) // rows_per
    j = lax.broadcasted_iota(jnp.int32, whole.shape, 1) // cols_per
    return halves(jnp.where(i == j, whole, 0.0))


def encode_tables(pat, wenc, lenc):
    down, across = pat[:TILE], pat[TILE:]
    hi, lo = block_diagonal(down[:, :BCOL], GCOL // TILE, TILE, BAND)
    wenc[:, :BCOL] = hi
    wenc[:, BCOL:] = lo
    hi, lo = block_diagonal(across[:, :ROWS], ROWS // TILE, BAND, TILE)
    lenc[:BROW] = hi
    lenc[BROW:] = lo


def decode_tables(pat, wdec, ldec):
    down, across = pat[:TILE], pat[TILE:]
    hi, lo = block_diagonal(across, GCOL // TILE, BAND, TILE)
    wdec[:BCOL] = hi
    wdec[BCOL:2 * BCOL] = hi
    wdec[2 * BCOL:] = lo
    hi, lo = block_diagonal(down[:, :BROW], ROWS // TILE, TILE, BAND)
    ldec[...] = jnp.concatenate([hi, hi, lo], axis=1)


def halves(a):
    hi = a.astype(BF16)
    return hi, (a - hi.astype(F32)).astype(BF16)


def dot(a, b):
    return jnp.dot(a, b, preferred_element_type=F32)


def decode_group(band, w_dec, l_dec):
    hi, lo = halves(band)
    wide = dot(jnp.concatenate([hi, lo, hi], axis=1), w_dec)
    hi, lo = halves(wide)
    return dot(l_dec, jnp.concatenate([hi, lo, hi], axis=0))


def group_of(plane):
    return plane - lax.div(plane, IDLE + 1)


def far(k, n):
    return n // 2 + lax.div(k + 1, 2) * (1 - 2 * lax.rem(k, 2))


def drain(buf, count, sem):
    part = buf.at[pl.ds(0, count)]
    pltpu.make_async_copy(part, part, sem).wait()


def sync_kernel(
    m_hbm, g_hbm, pat_hbm,
    nm, upd,
    m_v, g_v, pat, wenc, lenc, wdec, ldec, xs, xr, zs, zr, abuf, wide, sq1, sq2, scales,
    g_sem, m_sem, c_sem, p1_send, p1_recv, p2_send, p2_recv, x_send, x_recv, z_send, z_recv, a_send, a_recv,
):
    rep = lax.axis_index("replica")
    ten = lax.axis_index("tensor")
    z, x = lax.div(rep, NX), lax.rem(rep, NX)
    y, c = lax.div(ten, NC), lax.rem(ten, NC)

    def plane_peer(k):
        dx, dy, dc = far(lax.div(k, NY * NC), NX), far(lax.rem(lax.div(k, NC), NY), NY), far(lax.rem(k, NC), NC)
        return {
            "replica": z * NX + lax.rem(x + dx, NX),
            "tensor": lax.rem(y + dy, NY) * NC + lax.rem(c + dc, NC),
        }

    def z_peer(d):
        return {"replica": lax.rem(z + d, NZ) * NX + x}

    def x_peer(d):
        return {"replica": z * NX + lax.rem(x + d, NX)}

    def replica_peer(k):
        dz, dx = far(lax.div(k, NX), NZ), far(lax.rem(k, NX), NX)
        return {"replica": lax.rem(z + dz, NZ) * NX + lax.rem(x + dx, NX)}

    def send(src, dst, send_sem, recv_sem, peer):
        pltpu.make_async_remote_copy(
            src_ref=src, dst_ref=dst, send_sem=send_sem, recv_sem=recv_sem, device_id=peer, device_id_type=MESH
        ).start()

    def grad_copy(g, width):
        return pltpu.make_async_copy(
            g_hbm.at[0, :, :, pl.ds(g * GCOL, width)], g_v.at[g, :, :, pl.ds(0, width)], g_sem.at[g]
        )

    def mom_copy(g, width):
        return pltpu.make_async_copy(
            m_hbm.at[0, :, pl.ds(g * GCOL, width)], m_v.at[g, :, pl.ds(0, width)], m_sem.at[g]
        )

    pattern = pltpu.make_async_copy(pat_hbm, pat, c_sem)
    pattern.start()
    widths = [GCOL] * (GROUPS - 1) + [LAST]
    for g in range(GROUPS):
        grad_copy(g, widths[g]).start()

    barrier = pltpu.get_barrier_semaphore()

    def greet_z(k, _):
        pl.semaphore_signal(barrier, inc=1, device_id=z_peer(far(k, NZ)), device_id_type=MESH)
        return 0

    def greet_plane(k, _):
        pl.semaphore_signal(barrier, inc=1, device_id=plane_peer(k), device_id_type=MESH)
        return 0

    lax.fori_loop(0, NZ - 1, greet_z, 0)
    lax.fori_loop(0, PLANE - 1, greet_plane, 0)

    pattern.wait()
    encode_tables(pat, wenc, lenc)

    m_v[GROUPS - 1, :, LAST:] = jnp.zeros((ROWS, GCOL - LAST), F32)
    g_v[GROUPS - 1, :, :, LAST:] = jnp.zeros((STEPS, ROWS, GCOL - LAST), BF16)

    def squares(g, sums):
        def rows(i, sums):
            at = pl.ds(pl.multiple_of(i * 16, 16), 16)
            x0 = g_v[g, 0, at, :].astype(F32)
            x1 = g_v[g, 1, at, :].astype(F32)
            return sums[0] + x0 * x0, sums[1] + x1 * x1

        return lax.fori_loop(0, ROWS // 16, rows, sums, unroll=4)

    def waited(g, sums):
        grad_copy(g, GCOL).wait()
        mom_copy(g, GCOL).start()
        return squares(g, sums)

    sums = (jnp.zeros((16, GCOL), F32), jnp.zeros((16, GCOL), F32))
    sums = lax.fori_loop(0, GROUPS - 1, waited, sums)
    grad_copy(GROUPS - 1, LAST).wait()
    mom_copy(GROUPS - 1, LAST).start()
    sums = squares(GROUPS - 1, sums)

    def lanes(v):
        v = jnp.sum(v, axis=0, keepdims=True)
        return v[:, :128] + v[:, 128:256] + v[:, 256:384] + v[:, 384:]

    here = (x * NY + y) * NC + c
    sq1[here] = jnp.concatenate([lanes(sums[0]), lanes(sums[1])], axis=0)
    pl.semaphore_wait(barrier, NZ - 1 + PLANE - 1)

    def send_plane(k, _):
        send(sq1.at[here], sq1.at[here], p1_send, p1_recv, plane_peer(k))
        return 0

    lax.fori_loop(0, PLANE - 1, send_plane, 0)

    def encode_group(g):
        m_hi, m_lo = halves(m_v[g])
        w = wenc[...]
        cols = [dot(m_hi, w) + dot(m_lo, w)]
        for s in range(STEPS):
            cols.append(dot(g_v[g, s], w))
        wide = jnp.concatenate([v[:, :BCOL] + v[:, BCOL:] for v in cols], axis=1)
        hi, lo = halves(wide)
        first = dot(lenc[...], hi)
        e = first[:BROW] + first[BROW:] + dot(lenc[:BROW], lo)
        for i in range(STEPS + 1):
            xs[:, g, i] = e[:, i * BCOL:(i + 1) * BCOL].reshape(NX, QUART, BCOL)

    def send_quarters(g):
        for d in (2, 1, 3):
            send(xs.at[lax.rem(x + d, NX), g], xr.at[d - 1, g], x_send, x_recv, x_peer(d))

    def encode_waited(g, _):
        mom_copy(g, GCOL).wait()
        encode_group(g)
        send_quarters(g)
        return 0

    lax.fori_loop(0, GROUPS - 1, encode_waited, 0)
    mom_copy(GROUPS - 1, LAST).wait()
    encode_group(GROUPS - 1)
    send_quarters(GROUPS - 1)

    drain(sq1, PLANE - 1, p1_recv)
    sq2[z] = jnp.sum(sq1[...], axis=0)

    def send_z(k, _):
        send(sq2.at[z], sq2.at[z], p2_send, p2_recv, z_peer(far(k, NZ)))
        return 0

    lax.fori_loop(0, NZ - 1, send_z, 0)

    decode_tables(pat, wdec, ldec)

    drain(xr, NX - 1, x_recv)
    mine = xs[x] + xr[0] + xr[1] + xr[2]

    drain(sq2, NZ - 1, p2_recv)
    total = jnp.sum(jnp.sum(sq2[...], axis=0), axis=1, keepdims=True)
    total = jnp.broadcast_to(total, (STEPS, 128))
    count = float(REP * ROWS * TEN * COLS)
    scale = jnp.minimum(1.0, CLIP / jnp.sqrt(total / count + EPS))
    scales[...] = scale
    s0, s1 = scale[0:1], scale[1:2]
    zs[...] = BETA * mine[:, 0] + s0 * mine[:, 1] + s1 * mine[:, 2]

    def send_group(k, _):
        d = far(k, NZ)
        peer = lax.rem(z + d, NZ)

        @pl.when(peer != IDLE)
        def _():
            send(zs.at[group_of(peer)], zr.at[d - 1], z_send, z_recv, z_peer(d))

        return 0

    lax.fori_loop(0, NZ - 1, send_group, 0)

    def momentum_group(g, _):
        sc = scales[...]
        t0, t1 = sc[0:1], sc[1:2]
        own = BETA * (BETA * xs[:, g, 0] + t0 * xs[:, g, 1]) + t1 * xs[:, g, 2]
        low = decode_group(own.reshape(BROW, BCOL), wdec[...], ldec[...])
        state = BETA * m_v[g] + t0[:, 0:1] * g_v[g, 0].astype(F32)
        nm[g] = BETA * state + t1[:, 0:1] * g_v[g, 1].astype(F32) - low
        return 0

    lax.fori_loop(0, 3, momentum_group, 0)

    owner = z != IDLE
    mine_g = group_of(z)

    @pl.when(owner)
    def _():
        drain(zr, NZ - 1, z_recv)
        own = abuf.at[mine_g * NX + x]
        own[...] = zs[mine_g] + jnp.sum(zr[...], axis=0)

        def send_sum(k, _):
            peer = lax.div(k, NX) * NX + lax.rem(x + lax.rem(k, NX), NX)

            @pl.when(peer != rep)
            def _():
                send(own, own, a_send, a_recv, {"replica": peer})

            return 0

        lax.fori_loop(0, REP, send_sum, 0)

    lax.fori_loop(3, GROUPS, momentum_group, 0)

    @pl.when(owner)
    def _():
        drain(abuf, PIECES - 1, a_recv)

    @pl.when(jnp.logical_not(owner))
    def _():
        drain(abuf, PIECES, a_recv)

    hi, lo = halves(abuf[...].reshape(GROUPS * BROW, BCOL))
    wide[...] = dot(jnp.concatenate([hi, lo, hi], axis=1), wdec[...])
    for g in range(GROUPS):
        hi, lo = halves(wide[g * BROW:(g + 1) * BROW])
        upd[g] = dot(ldec[...], jnp.concatenate([hi, lo, hi], axis=0)).astype(BF16)

    drain(sq1, PLANE - 1, p1_send)
    drain(sq2, NZ - 1, p2_send)
    drain(xr, NX - 1, x_send)

    @pl.when(owner)
    def _():
        drain(zs, GROUPS - 1, z_send)
        drain(abuf, PIECES, a_send)
        drain(abuf, REP - 1 - PIECES, a_send)

    @pl.when(jnp.logical_not(owner))
    def _():
        drain(zs, GROUPS, z_send)


def write_kernel(nm, upd, out_m, out_u, m_sem, u_sem):
    copies = []
    for g in range(GROUPS):
        width = GCOL if g < GROUPS - 1 else LAST
        here, there = pl.ds(0, width), pl.ds(g * GCOL, width)
        copies.append(pltpu.make_async_copy(nm.at[g, :, here], out_m.at[0, :, there], m_sem.at[g]))
        copies.append(pltpu.make_async_copy(upd.at[g, :, here], out_u.at[:, there], u_sem.at[g]))
    for copy in copies:
        copy.start()
    for copy in copies:
        copy.wait()


def per_device(momentum, grads):
    table = jnp.asarray(patterns())
    hbm = pl.BlockSpec(memory_space=pl.ANY)
    vmem = pl.BlockSpec(memory_space=pltpu.VMEM)
    dma = pltpu.SemaphoreType.DMA
    nm, upd = pl.pallas_call(
        sync_kernel,
        out_shape=(
            pltpu.VMEM((GROUPS, ROWS, GCOL), F32),
            pltpu.VMEM((GROUPS, ROWS, GCOL), BF16),
        ),
        in_specs=[hbm] * 3,
        out_specs=(vmem,) * 2,
        scratch_shapes=[
            pltpu.VMEM((GROUPS, ROWS, GCOL), F32),
            pltpu.VMEM((GROUPS, STEPS, ROWS, GCOL), BF16),
            pltpu.VMEM((TILE + BAND, GCOL), F32),
            pltpu.VMEM((GCOL, 2 * BCOL), BF16),
            pltpu.VMEM((2 * BROW, ROWS), BF16),
            pltpu.VMEM((3 * BCOL, GCOL), BF16),
            pltpu.VMEM((ROWS, 3 * BROW), BF16),
            pltpu.VMEM((NX, GROUPS, STEPS + 1, QUART, BCOL), F32),
            pltpu.VMEM((NX - 1, GROUPS, STEPS + 1, QUART, BCOL), F32),
            pltpu.VMEM((GROUPS, QUART, BCOL), F32),
            pltpu.VMEM((NZ - 1, QUART, BCOL), F32),
            pltpu.VMEM((PIECES, QUART, BCOL), F32),
            pltpu.VMEM((GROUPS * BROW, GCOL), F32),
            pltpu.VMEM((PLANE, STEPS, 128), F32),
            pltpu.VMEM((NZ, STEPS, 128), F32),
            pltpu.VMEM((STEPS, 128), F32),
            dma((GROUPS,)), dma((GROUPS,)), dma,
            dma, dma, dma, dma, dma, dma, dma, dma, dma, dma,
        ],
        compiler_params=pltpu.CompilerParams(
            collective_id=0, has_side_effects=True, vmem_limit_bytes=36 * 1024 * 1024
        ),
        name="sync",
    )(*(pltpu.with_memory_space_constraint(a, pltpu.HBM) for a in (momentum, grads, table)))
    return pl.pallas_call(
        write_kernel,
        out_shape=(
            jax.ShapeDtypeStruct((1, ROWS, COLS), F32),
            jax.ShapeDtypeStruct((ROWS, COLS), BF16),
        ),
        in_specs=[vmem] * 2,
        out_specs=(hbm, hbm),
        scratch_shapes=[dma((GROUPS,)), dma((GROUPS,))],
        compiler_params=pltpu.CompilerParams(vmem_limit_bytes=8 * 1024 * 1024),
        name="write",
    )(*(pltpu.with_memory_space_constraint(a, pltpu.VMEM) for a in (nm, upd)))


def solution(mesh):
    in_specs = (P("replica", None, "tensor"), P("replica", None, None, "tensor"))
    out_specs = (P("replica", None, "tensor"), P(None, "tensor"))
    return jax.shard_map(
        per_device, mesh=mesh, in_specs=in_specs, out_specs=out_specs, check_vma=False
    )
```

```python
import itertools
import math

import jax
import jax.numpy as jnp
import ml_dtypes
import numpy as np
from jax import lax
from jax.experimental import pallas as pl
from jax.experimental.pallas import tpu as pltpu
from jax.sharding import PartitionSpec as P

TILE = 32
BAND = 8
STEPS = 2
BETA = 0.9
CLIP = 1.0
EPS = 1e-06

MESH = pl.DeviceIdType.MESH
F32 = jnp.float32
BF16 = jnp.bfloat16

REP = 32
TEN = 8
NX, NY, NZ, NC = 4, 4, 8, 2
PLANE = NX * NY * NC
BEFORE = 3
IDLE = 4
ROWS = 256
COLS = 3456
GCOL = 512
GROUPS = 7
LAST = COLS - (GROUPS - 1) * GCOL
BROW = ROWS // TILE * BAND
BCOL = GCOL // TILE * BAND
QUART = 16
PIECES = GROUPS * (BROW // QUART)


def patterns():
    freq = np.arange(BAND, dtype=np.float64)[:, None]
    place = np.arange(TILE, dtype=np.float64)[None, :]
    weight = np.where(freq == 0, math.sqrt(1.0 / TILE), math.sqrt(2.0 / TILE))
    low = weight * np.cos(math.pi * (2.0 * place + 1.0) * freq / (2.0 * TILE))
    down = np.tile(low.T, (1, GCOL // BAND))
    across = np.tile(low, (1, GCOL // TILE))
    return np.concatenate([down, across], axis=0).astype(np.float32)


def block_diagonal(pattern, times, rows_per, cols_per):
    whole = jnp.concatenate([pattern] * times, axis=0)
    i = lax.broadcasted_iota(jnp.int32, whole.shape, 0) // rows_per
    j = lax.broadcasted_iota(jnp.int32, whole.shape, 1) // cols_per
    return halves(jnp.where(i == j, whole, 0.0))


def encode_tables(pat, wenc, lenc):
    down, across = pat[:TILE], pat[TILE:]
    hi, lo = block_diagonal(down[:, :BCOL], GCOL // TILE, TILE, BAND)
    wenc[:, :BCOL] = hi
    wenc[:, BCOL:] = lo
    hi, lo = block_diagonal(across[:, :ROWS], ROWS // TILE, BAND, TILE)
    lenc[:BROW] = hi
    lenc[BROW:] = lo


def decode_tables(pat, wdec, ldec):
    down, across = pat[:TILE], pat[TILE:]
    hi, lo = block_diagonal(across, GCOL // TILE, BAND, TILE)
    wdec[:BCOL] = hi
    wdec[BCOL:2 * BCOL] = hi
    wdec[2 * BCOL:] = lo
    hi, lo = block_diagonal(down[:, :BROW], ROWS // TILE, TILE, BAND)
    ldec[...] = jnp.concatenate([hi, hi, lo], axis=1)


def halves(a):
    hi = a.astype(BF16)
    return hi, (a - hi.astype(F32)).astype(BF16)


def dot(a, b):
    return jnp.dot(a, b, preferred_element_type=F32)


def decode_group(band, w_dec, l_dec):
    hi, lo = halves(band)
    wide = dot(jnp.concatenate([hi, lo, hi], axis=1), w_dec)
    hi, lo = halves(wide)
    return dot(l_dec, jnp.concatenate([hi, lo, hi], axis=0))


def group_of(plane):
    return plane - lax.div(plane, IDLE + 1)


def plane_of(group):
    return group + lax.div(group, IDLE)


def far(n):
    return sorted(range(n), key=lambda d: -min(d, n - d))


def drain(buf, count, sem):
    part = buf.at[pl.ds(0, count)]
    pltpu.make_async_copy(part, part, sem).wait()


def sync_kernel(
    m_hbm, g_hbm, pat_hbm,
    nm, upd,
    m_v, g_v, pat, wenc, lenc, wdec, ldec, xs, xr, zs, zr, abuf, wide, sq1, sq2, scales,
    g_sem, m_sem, c_sem, p1_send, p1_recv, p2_send, p2_recv, x_send, x_recv, z_send, z_recv, a_send, a_recv,
):
    rep = lax.axis_index("replica")
    ten = lax.axis_index("tensor")
    z, x = lax.div(rep, NX), lax.rem(rep, NX)
    y, c = lax.div(ten, NC), lax.rem(ten, NC)

    zd = [lax.rem(z + d, NZ) for d in range(NZ)]
    xd = [lax.rem(x + d, NX) for d in range(NX)]
    yd = [lax.rem(y + d, NY) * NC for d in range(NY)]
    cd = [c, 1 - c]
    rows = z * NX
    plane_peers = [
        {"replica": rows + xd[dx], "tensor": yd[dy] + cd[dc]}
        for dx, dy, dc in sorted(
            itertools.product(range(NX), range(NY), range(NC)),
            key=lambda d: -(min(d[0], NX - d[0]) + min(d[1], NY - d[1])),
        )
        if dx or dy or dc
    ]
    z_peers = {d: {"replica": zd[d] * NX + x} for d in range(1, NZ)}
    x_peers = {d: {"replica": rows + xd[d]} for d in range(1, NX)}

    def send(src, dst, send_sem, recv_sem, peer):
        pltpu.make_async_remote_copy(
            src_ref=src, dst_ref=dst, send_sem=send_sem, recv_sem=recv_sem, device_id=peer, device_id_type=MESH
        ).start()

    def grad_copy(g, width):
        return pltpu.make_async_copy(
            g_hbm.at[0, :, :, pl.ds(g * GCOL, width)], g_v.at[g, :, :, pl.ds(0, width)], g_sem.at[g]
        )

    def mom_copy(g, width):
        return pltpu.make_async_copy(
            m_hbm.at[0, :, pl.ds(g * GCOL, width)], m_v.at[g, :, pl.ds(0, width)], m_sem.at[g]
        )

    pattern = pltpu.make_async_copy(pat_hbm, pat, c_sem)
    pattern.start()
    widths = [GCOL] * (GROUPS - 1) + [LAST]
    for g in range(GROUPS):
        grad_copy(g, widths[g]).start()

    barrier = pltpu.get_barrier_semaphore()

    greeted = [z_peers[d] for d in far(NZ)[:-1]]
    for peer in plane_peers[:8] + greeted + plane_peers[8:]:
        pl.semaphore_signal(barrier, inc=1, device_id=peer, device_id_type=MESH)

    pattern.wait()
    encode_tables(pat, wenc, lenc)

    m_v[GROUPS - 1, :, LAST:] = jnp.zeros((ROWS, GCOL - LAST), F32)
    g_v[GROUPS - 1, :, :, LAST:] = jnp.zeros((STEPS, ROWS, GCOL - LAST), BF16)

    def squares(g, sums):
        def rows(i, sums):
            at = pl.ds(pl.multiple_of(i * 16, 16), 16)
            x0 = g_v[g, 0, at, :].astype(F32)
            x1 = g_v[g, 1, at, :].astype(F32)
            return sums[0] + x0 * x0, sums[1] + x1 * x1

        return lax.fori_loop(0, ROWS // 16, rows, sums, unroll=4)

    def waited(g, sums):
        grad_copy(g, GCOL).wait()
        mom_copy(g, GCOL).start()
        return squares(g, sums)

    sums = (jnp.zeros((16, GCOL), F32), jnp.zeros((16, GCOL), F32))
    sums = lax.fori_loop(0, GROUPS - 1, waited, sums)
    grad_copy(GROUPS - 1, LAST).wait()
    mom_copy(GROUPS - 1, LAST).start()
    sums = squares(GROUPS - 1, sums)

    def lanes(v):
        v = jnp.sum(v, axis=0, keepdims=True)
        return v[:, :128] + v[:, 128:256] + v[:, 256:384] + v[:, 384:]

    here = (x * NY + y) * NC + c
    sq1[here] = jnp.concatenate([lanes(sums[0]), lanes(sums[1])], axis=0)
    def encode_group(g):
        m_hi, m_lo = halves(m_v[g])
        w = wenc[...]
        cols = [dot(m_hi, w) + dot(m_lo, w)]
        for s in range(STEPS):
            cols.append(dot(g_v[g, s], w))
        wide = jnp.concatenate([v[:, :BCOL] + v[:, BCOL:] for v in cols], axis=1)
        hi, lo = halves(wide)
        first = dot(lenc[...], hi)
        e = first[:BROW] + first[BROW:] + dot(lenc[:BROW], lo)
        for i in range(STEPS + 1):
            xs[:, g, i] = e[:, i * BCOL:(i + 1) * BCOL].reshape(NX, QUART, BCOL)

    def send_quarters(g):
        for d in (2, 1, 3):
            send(xs.at[xd[d], g], xr.at[d - 1, g], x_send, x_recv.at[g], x_peers[d])

    mine_g = group_of(z)

    def turn(k):
        return lax.rem(mine_g + 1 + k, GROUPS)

    def encode_waited(k):
        g = turn(k)

        @pl.when(g < GROUPS - 1)
        def _():
            mom_copy(g, GCOL).wait()

        @pl.when(g == GROUPS - 1)
        def _():
            mom_copy(GROUPS - 1, LAST).wait()

        encode_group(g)
        return g

    def encode_send(k, _):
        send_quarters(encode_waited(k))
        return 0

    ready = encode_waited(0)

    pl.semaphore_wait(barrier, NZ - 1 + PLANE - 1)

    for peer in plane_peers:
        send(sq1.at[here], sq1.at[here], p1_send, p1_recv, peer)

    send_quarters(ready)
    lax.fori_loop(1, GROUPS, encode_send, 0)

    def relay(k, _):
        g = turn(k)
        part = xr.at[:, g]
        pltpu.make_async_copy(part, part, x_recv.at[g]).wait()
        zs[g] = xs[x, g] + xr[0, g] + xr[1, g] + xr[2, g]
        plane = plane_of(g)

        @pl.when(plane != z)
        def _():
            d = lax.rem(plane + NZ - z, NZ)
            send(zs.at[g], zr.at[d - 1], z_send, z_recv, {"replica": plane * NX + x})

        return 0

    lax.fori_loop(0, BEFORE, relay, 0)

    drain(sq1, PLANE - 1, p1_recv)
    sq2[z] = jnp.sum(sq1[...], axis=0)

    for d in far(NZ)[:-1]:
        send(sq2.at[z], sq2.at[z], p2_send, p2_recv, z_peers[d])


    decode_tables(pat, wdec, ldec)

    lax.fori_loop(BEFORE, GROUPS, relay, 0)

    drain(sq2, NZ - 1, p2_recv)
    total = jnp.sum(jnp.sum(sq2[...], axis=0), axis=1, keepdims=True)
    total = jnp.broadcast_to(total, (STEPS, 128))
    count = float(REP * ROWS * TEN * COLS)
    scale = jnp.minimum(1.0, CLIP / jnp.sqrt(total / count + EPS))
    scales[...] = scale

    def momentum_group(g, _):
        sc = scales[...]
        t0, t1 = sc[0:1], sc[1:2]
        own = BETA * (BETA * xs[:, g, 0] + t0 * xs[:, g, 1]) + t1 * xs[:, g, 2]
        low = decode_group(own.reshape(BROW, BCOL), wdec[...], ldec[...])
        state = BETA * m_v[g] + t0[:, 0:1] * g_v[g, 0].astype(F32)
        nm[g] = BETA * state + t1[:, 0:1] * g_v[g, 1].astype(F32) - low
        return 0

    owner = z != IDLE

    @pl.when(owner)
    def _():
        drain(zr, NZ - 1, z_recv)
        own = abuf.at[mine_g * NX + x]
        whole = zs[mine_g] + jnp.sum(zr[...], axis=0)
        own[...] = BETA * whole[0] + scale[0:1] * whole[1] + scale[1:2] * whole[2]

        for plane in range(NZ):
            for d in range(1, NX):
                send(own, own, a_send, a_recv, {"replica": plane * NX + xd[d]})

            @pl.when(plane != z)
            def _():
                send(own, own, a_send, a_recv, {"replica": plane * NX + x})

    lax.fori_loop(0, GROUPS, momentum_group, 0)

    @pl.when(owner)
    def _():
        drain(abuf, PIECES - 1, a_recv)

    @pl.when(jnp.logical_not(owner))
    def _():
        drain(abuf, PIECES, a_recv)

    hi, lo = halves(abuf[...].reshape(GROUPS * BROW, BCOL))
    wide[...] = dot(jnp.concatenate([hi, lo, hi], axis=1), wdec[...])
    for g in range(GROUPS):
        hi, lo = halves(wide[g * BROW:(g + 1) * BROW])
        upd[g] = dot(ldec[...], jnp.concatenate([hi, lo, hi], axis=0)).astype(BF16)

    drain(sq1, PLANE - 1, p1_send)
    drain(sq2, NZ - 1, p2_send)
    drain(xr, NX - 1, x_send)

    @pl.when(owner)
    def _():
        drain(zs, GROUPS - 1, z_send)
        drain(abuf, PIECES, a_send)
        drain(abuf, REP - 1 - PIECES, a_send)

    @pl.when(jnp.logical_not(owner))
    def _():
        drain(zs, GROUPS, z_send)


def write_kernel(nm, upd, out_m, out_u, m_sem, u_sem):
    copies = []
    for g in range(GROUPS):
        width = GCOL if g < GROUPS - 1 else LAST
        here, there = pl.ds(0, width), pl.ds(g * GCOL, width)
        copies.append(pltpu.make_async_copy(nm.at[g, :, here], out_m.at[0, :, there], m_sem.at[g]))
        copies.append(pltpu.make_async_copy(upd.at[g, :, here], out_u.at[:, there], u_sem.at[g]))
    for copy in copies:
        copy.start()
    for copy in copies:
        copy.wait()


def per_device(momentum, grads):
    table = jnp.asarray(patterns())
    hbm = pl.BlockSpec(memory_space=pl.ANY)
    vmem = pl.BlockSpec(memory_space=pltpu.VMEM)
    dma = pltpu.SemaphoreType.DMA
    nm, upd = pl.pallas_call(
        sync_kernel,
        out_shape=(
            pltpu.VMEM((GROUPS, ROWS, GCOL), F32),
            pltpu.VMEM((GROUPS, ROWS, GCOL), BF16),
        ),
        in_specs=[hbm] * 3,
        out_specs=(vmem,) * 2,
        scratch_shapes=[
            pltpu.VMEM((GROUPS, ROWS, GCOL), F32),
            pltpu.VMEM((GROUPS, STEPS, ROWS, GCOL), BF16),
            pltpu.VMEM((TILE + BAND, GCOL), F32),
            pltpu.VMEM((GCOL, 2 * BCOL), BF16),
            pltpu.VMEM((2 * BROW, ROWS), BF16),
            pltpu.VMEM((3 * BCOL, GCOL), BF16),
            pltpu.VMEM((ROWS, 3 * BROW), BF16),
            pltpu.VMEM((NX, GROUPS, STEPS + 1, QUART, BCOL), F32),
            pltpu.VMEM((NX - 1, GROUPS, STEPS + 1, QUART, BCOL), F32),
            pltpu.VMEM((GROUPS, STEPS + 1, QUART, BCOL), F32),
            pltpu.VMEM((NZ - 1, STEPS + 1, QUART, BCOL), F32),
            pltpu.VMEM((PIECES, QUART, BCOL), F32),
            pltpu.VMEM((GROUPS * BROW, GCOL), F32),
            pltpu.VMEM((PLANE, STEPS, 128), F32),
            pltpu.VMEM((NZ, STEPS, 128), F32),
            pltpu.VMEM((STEPS, 128), F32),
            dma((GROUPS,)), dma((GROUPS,)), dma,
            dma, dma, dma, dma, dma, dma((GROUPS,)), dma, dma, dma, dma,
        ],
        compiler_params=pltpu.CompilerParams(
            collective_id=0, has_side_effects=True, vmem_limit_bytes=36 * 1024 * 1024
        ),
        name="sync",
    )(*(pltpu.with_memory_space_constraint(a, pltpu.HBM) for a in (momentum, grads, table)))
    return pl.pallas_call(
        write_kernel,
        out_shape=(
            jax.ShapeDtypeStruct((1, ROWS, COLS), F32),
            jax.ShapeDtypeStruct((ROWS, COLS), BF16),
        ),
        in_specs=[vmem] * 2,
        out_specs=(hbm, hbm),
        scratch_shapes=[dma((GROUPS,)), dma((GROUPS,))],
        compiler_params=pltpu.CompilerParams(vmem_limit_bytes=8 * 1024 * 1024),
        name="write",
    )(*(pltpu.with_memory_space_constraint(a, pltpu.VMEM) for a in (nm, upd)))


def solution(mesh):
    in_specs = (P("replica", None, "tensor"), P("replica", None, None, "tensor"))
    out_specs = (P("replica", None, "tensor"), P(None, "tensor"))
    return jax.shard_map(
        per_device, mesh=mesh, in_specs=in_specs, out_specs=out_specs, check_vma=False
    )
```

```python
import itertools
import math

import jax
import jax.numpy as jnp
import ml_dtypes
import numpy as np
from jax import lax
from jax.experimental import pallas as pl
from jax.experimental.pallas import tpu as pltpu
from jax.sharding import PartitionSpec as P

TILE = 32
BAND = 8
STEPS = 2
BETA = 0.9
CLIP = 1.0
EPS = 1e-06

MESH = pl.DeviceIdType.MESH
F32 = jnp.float32
BF16 = jnp.bfloat16

REP = 32
TEN = 8
NX, NY, NZ, NC = 4, 4, 8, 2
PLANE = NX * NY * NC
BATCHES = ((0, 6, 5, 4), (1, 2, 3))
BEFORE = 3
IDLE = 4
ROWS = 256
COLS = 3456
GCOL = 512
GROUPS = 7
LAST = COLS - (GROUPS - 1) * GCOL
BROW = ROWS // TILE * BAND
BCOL = GCOL // TILE * BAND
QUART = 16
PIECES = GROUPS * (BROW // QUART)


def patterns():
    freq = np.arange(BAND, dtype=np.float64)[:, None]
    place = np.arange(TILE, dtype=np.float64)[None, :]
    weight = np.where(freq == 0, math.sqrt(1.0 / TILE), math.sqrt(2.0 / TILE))
    low = weight * np.cos(math.pi * (2.0 * place + 1.0) * freq / (2.0 * TILE))
    down = np.tile(low.T, (1, GCOL // BAND))
    across = np.tile(low, (1, GCOL // TILE))
    return np.concatenate([down, across], axis=0).astype(np.float32)


def block_diagonal(pattern, times, rows_per, cols_per):
    whole = jnp.concatenate([pattern] * times, axis=0)
    i = lax.broadcasted_iota(jnp.int32, whole.shape, 0) // rows_per
    j = lax.broadcasted_iota(jnp.int32, whole.shape, 1) // cols_per
    return halves(jnp.where(i == j, whole, 0.0))


def encode_tables(pat, wenc, lenc):
    down, across = pat[:TILE], pat[TILE:]
    hi, lo = block_diagonal(down[:, :BCOL], GCOL // TILE, TILE, BAND)
    wenc[:, :BCOL] = hi
    wenc[:, BCOL:] = lo
    hi, lo = block_diagonal(across[:, :ROWS], ROWS // TILE, BAND, TILE)
    lenc[:BROW] = hi
    lenc[BROW:] = lo


def decode_tables(pat, wdec, ldec):
    down, across = pat[:TILE], pat[TILE:]
    hi, lo = block_diagonal(across, GCOL // TILE, BAND, TILE)
    wdec[:BCOL] = hi
    wdec[BCOL:2 * BCOL] = hi
    wdec[2 * BCOL:] = lo
    hi, lo = block_diagonal(down[:, :BROW], ROWS // TILE, TILE, BAND)
    ldec[...] = jnp.concatenate([hi, hi, lo], axis=1)


def halves(a):
    hi = a.astype(BF16)
    return hi, (a - hi.astype(F32)).astype(BF16)


def dot(a, b):
    return jnp.dot(a, b, preferred_element_type=F32)


def decode_group(band, w_dec, l_dec):
    hi, lo = halves(band)
    wide = dot(jnp.concatenate([hi, lo, hi], axis=1), w_dec)
    hi, lo = halves(wide)
    return dot(l_dec, jnp.concatenate([hi, lo, hi], axis=0))


def group_of(plane):
    return plane - lax.div(plane, IDLE + 1)


def plane_of(group):
    return group + group // IDLE


def far(n):
    return sorted(range(n), key=lambda d: -min(d, n - d))


def drain(buf, count, sem):
    part = buf.at[pl.ds(0, count)]
    pltpu.make_async_copy(part, part, sem).wait()


def sync_kernel(
    m_hbm, g_hbm, pat_hbm,
    nm, upd,
    m_v, g_v, pat, wenc, lenc, wdec, ldec, xs, xr, zs, zr, abuf, wide, sq1, sq2, scales,
    g_sem, m_sem, c_sem, p1_send, p1_recv, p2_send, p2_recv, x_send, x_recv, z_send, z_recv, a_send, a_recv,
):
    rep = lax.axis_index("replica")
    ten = lax.axis_index("tensor")
    z, x = lax.div(rep, NX), lax.rem(rep, NX)
    y, c = lax.div(ten, NC), lax.rem(ten, NC)

    zd = [lax.rem(z + d, NZ) for d in range(NZ)]
    xd = [lax.rem(x + d, NX) for d in range(NX)]
    yd = [lax.rem(y + d, NY) * NC for d in range(NY)]
    cd = [c, 1 - c]
    rows = z * NX
    plane_peers = [
        {"replica": rows + xd[dx], "tensor": yd[dy] + cd[dc]}
        for dx, dy, dc in sorted(
            itertools.product(range(NX), range(NY), range(NC)),
            key=lambda d: -(min(d[0], NX - d[0]) + min(d[1], NY - d[1])),
        )
        if dx or dy or dc
    ]
    z_peers = {d: {"replica": zd[d] * NX + x} for d in range(1, NZ)}
    x_peers = {d: {"replica": rows + xd[d]} for d in range(1, NX)}

    def send(src, dst, send_sem, recv_sem, peer):
        pltpu.make_async_remote_copy(
            src_ref=src, dst_ref=dst, send_sem=send_sem, recv_sem=recv_sem, device_id=peer, device_id_type=MESH
        ).start()

    def grad_copy(g, width):
        return pltpu.make_async_copy(
            g_hbm.at[0, :, :, pl.ds(g * GCOL, width)], g_v.at[g, :, :, pl.ds(0, width)], g_sem.at[g]
        )

    def mom_copy(g, width):
        return pltpu.make_async_copy(
            m_hbm.at[0, :, pl.ds(g * GCOL, width)], m_v.at[g, :, pl.ds(0, width)], m_sem.at[g]
        )

    pattern = pltpu.make_async_copy(pat_hbm, pat, c_sem)
    pattern.start()
    widths = [GCOL] * (GROUPS - 1) + [LAST]
    barrier = pltpu.get_barrier_semaphore()

    greeted = [z_peers[d] for d in far(NZ)[:-1]]
    greeted = plane_peers[:8] + greeted + plane_peers[8:]
    for peer in greeted[:12]:
        pl.semaphore_signal(barrier, inc=1, device_id=peer, device_id_type=MESH)
    for g in range(GROUPS):
        grad_copy(g, widths[g]).start()

    for peer in greeted[12:]:
        pl.semaphore_signal(barrier, inc=1, device_id=peer, device_id_type=MESH)


    pattern.wait()
    encode_tables(pat, wenc, lenc)

    m_v[GROUPS - 1, :, LAST:] = jnp.zeros((ROWS, GCOL - LAST), F32)
    g_v[GROUPS - 1, :, :, LAST:] = jnp.zeros((STEPS, ROWS, GCOL - LAST), BF16)

    def squares(g, sums):
        def rows(i, sums):
            at = pl.ds(pl.multiple_of(i * 16, 16), 16)
            x0 = g_v[g, 0, at, :].astype(F32)
            x1 = g_v[g, 1, at, :].astype(F32)
            return sums[0] + x0 * x0, sums[1] + x1 * x1

        return lax.fori_loop(0, ROWS // 16, rows, sums, unroll=4)

    def waited(g, sums):
        grad_copy(g, GCOL).wait()
        mom_copy(g, GCOL).start()
        return squares(g, sums)

    sums = (jnp.zeros((16, GCOL), F32), jnp.zeros((16, GCOL), F32))
    sums = lax.fori_loop(0, GROUPS - 1, waited, sums)
    grad_copy(GROUPS - 1, LAST).wait()
    mom_copy(GROUPS - 1, LAST).start()
    sums = squares(GROUPS - 1, sums)

    def lanes(v):
        v = jnp.sum(v, axis=0, keepdims=True)
        return v[:, :128] + v[:, 128:256] + v[:, 256:384] + v[:, 384:]

    here = (x * NY + y) * NC + c
    sq1[here] = jnp.concatenate([lanes(sums[0]), lanes(sums[1])], axis=0)
    def encode_group(g):
        m_hi, m_lo = halves(m_v[g])
        w = wenc[...]
        cols = [dot(m_hi, w) + dot(m_lo, w)]
        for s in range(STEPS):
            cols.append(dot(g_v[g, s], w))
        wide = jnp.concatenate([v[:, :BCOL] + v[:, BCOL:] for v in cols], axis=1)
        hi, lo = halves(wide)
        first = dot(lenc[...], hi)
        e = first[:BROW] + first[BROW:] + dot(lenc[:BROW], lo)
        for i in range(STEPS + 1):
            xs[:, g, i] = e[:, i * BCOL:(i + 1) * BCOL].reshape(NX, QUART, BCOL)

    def send_quarters(g):
        for d in (2, 1, 3):
            send(xs.at[xd[d], g], xr.at[d - 1, g], x_send, x_recv.at[g], x_peers[d])

    mine_g = group_of(z)

    def turn(k):
        return lax.rem(mine_g + 1 + k, GROUPS)

    def encode_waited(k):
        g = turn(k)

        @pl.when(g < GROUPS - 1)
        def _():
            mom_copy(g, GCOL).wait()

        @pl.when(g == GROUPS - 1)
        def _():
            mom_copy(GROUPS - 1, LAST).wait()

        encode_group(g)
        return g

    def encode_send(k, _):
        send_quarters(encode_waited(k))
        return 0

    ready = encode_waited(0)

    pl.semaphore_wait(barrier, NZ - 1 + PLANE - 1)
    send_quarters(ready)

    for peer in plane_peers:
        send(sq1.at[here], sq1.at[here], p1_send, p1_recv, peer)

    lax.fori_loop(1, GROUPS, encode_send, 0)

    def relay(k, _):
        g = turn(k)
        part = xr.at[:, g]
        pltpu.make_async_copy(part, part, x_recv.at[g]).wait()
        zs[g] = xs[x, g] + xr[0, g] + xr[1, g] + xr[2, g]
        plane = plane_of(g)

        @pl.when(plane != z)
        def _():
            d = lax.rem(plane + NZ - z, NZ)
            send(zs.at[g], zr.at[d - 1], z_send, z_recv, {"replica": plane * NX + x})

        return 0

    lax.fori_loop(0, BEFORE, relay, 0)

    drain(sq1, PLANE - 1, p1_recv)
    sq2[z] = jnp.sum(sq1[...], axis=0)

    for d in far(NZ)[:-1]:
        send(sq2.at[z], sq2.at[z], p2_send, p2_recv, z_peers[d])


    decode_tables(pat, wdec, ldec)

    lax.fori_loop(BEFORE, GROUPS, relay, 0)

    drain(sq2, NZ - 1, p2_recv)
    total = jnp.sum(jnp.sum(sq2[...], axis=0), axis=1, keepdims=True)
    total = jnp.broadcast_to(total, (STEPS, 128))
    count = float(REP * ROWS * TEN * COLS)
    scale = jnp.minimum(1.0, CLIP / jnp.sqrt(total / count + EPS))
    scales[...] = scale

    def momentum_group(g, _):
        sc = scales[...]
        t0, t1 = sc[0:1], sc[1:2]
        own = BETA * (BETA * xs[:, g, 0] + t0 * xs[:, g, 1]) + t1 * xs[:, g, 2]
        low = decode_group(own.reshape(BROW, BCOL), wdec[...], ldec[...])
        state = BETA * m_v[g] + t0[:, 0:1] * g_v[g, 0].astype(F32)
        nm[g] = BETA * state + t1[:, 0:1] * g_v[g, 1].astype(F32) - low
        return 0

    owner = z != IDLE

    @pl.when(owner)
    def _():
        drain(zr, NZ - 1, z_recv)
        own = abuf.at[mine_g * NX + x]
        whole = zs[mine_g] + jnp.sum(zr[...], axis=0)
        own[...] = BETA * whole[0] + scale[0:1] * whole[1] + scale[1:2] * whole[2]

        for plane in range(NZ):
            for d in range(1, NX):
                send(own, own, a_send, a_recv.at[mine_g], {"replica": plane * NX + xd[d]})

            @pl.when(plane != z)
            def _():
                send(own, own, a_send, a_recv.at[mine_g], {"replica": plane * NX + x})

    lax.fori_loop(0, GROUPS, momentum_group, 0)

    def await_group(g):
        @pl.when(plane_of(g) == z)
        def _():
            drain(abuf, NX - 1, a_recv.at[g])

        @pl.when(plane_of(g) != z)
        def _():
            drain(abuf, NX, a_recv.at[g])

    for batch in BATCHES:
        for g in batch:
            await_group(g)
        parts = [abuf[g * NX:(g + 1) * NX].reshape(BROW, BCOL) for g in batch]
        hi, lo = halves(jnp.concatenate(parts, axis=0))
        wide[:len(batch) * BROW] = dot(jnp.concatenate([hi, lo, hi], axis=1), wdec[...])
        for i, g in enumerate(batch):
            hi, lo = halves(wide[i * BROW:(i + 1) * BROW])
            upd[g] = dot(ldec[...], jnp.concatenate([hi, lo, hi], axis=0)).astype(BF16)

    drain(sq1, PLANE - 1, p1_send)
    drain(sq2, NZ - 1, p2_send)
    drain(xr, NX - 1, x_send)

    @pl.when(owner)
    def _():
        drain(zs, GROUPS - 1, z_send)
        drain(abuf, PIECES, a_send)
        drain(abuf, REP - 1 - PIECES, a_send)

    @pl.when(jnp.logical_not(owner))
    def _():
        drain(zs, GROUPS, z_send)


def write_kernel(nm, upd, out_m, out_u, m_sem, u_sem):
    copies = []
    for g in range(GROUPS):
        width = GCOL if g < GROUPS - 1 else LAST
        here, there = pl.ds(0, width), pl.ds(g * GCOL, width)
        copies.append(pltpu.make_async_copy(nm.at[g, :, here], out_m.at[0, :, there], m_sem.at[g]))
        copies.append(pltpu.make_async_copy(upd.at[g, :, here], out_u.at[:, there], u_sem.at[g]))
    for copy in copies:
        copy.start()
    for copy in copies:
        copy.wait()


def per_device(momentum, grads):
    table = jnp.asarray(patterns())
    hbm = pl.BlockSpec(memory_space=pl.ANY)
    vmem = pl.BlockSpec(memory_space=pltpu.VMEM)
    dma = pltpu.SemaphoreType.DMA
    nm, upd = pl.pallas_call(
        sync_kernel,
        out_shape=(
            pltpu.VMEM((GROUPS, ROWS, GCOL), F32),
            pltpu.VMEM((GROUPS, ROWS, GCOL), BF16),
        ),
        in_specs=[hbm] * 3,
        out_specs=(vmem,) * 2,
        scratch_shapes=[
            pltpu.VMEM((GROUPS, ROWS, GCOL), F32),
            pltpu.VMEM((GROUPS, STEPS, ROWS, GCOL), BF16),
            pltpu.VMEM((TILE + BAND, GCOL), F32),
            pltpu.VMEM((GCOL, 2 * BCOL), BF16),
            pltpu.VMEM((2 * BROW, ROWS), BF16),
            pltpu.VMEM((3 * BCOL, GCOL), BF16),
            pltpu.VMEM((ROWS, 3 * BROW), BF16),
            pltpu.VMEM((NX, GROUPS, STEPS + 1, QUART, BCOL), F32),
            pltpu.VMEM((NX - 1, GROUPS, STEPS + 1, QUART, BCOL), F32),
            pltpu.VMEM((GROUPS, STEPS + 1, QUART, BCOL), F32),
            pltpu.VMEM((NZ - 1, STEPS + 1, QUART, BCOL), F32),
            pltpu.VMEM((PIECES, QUART, BCOL), F32),
            pltpu.VMEM((GROUPS * BROW, GCOL), F32),
            pltpu.VMEM((PLANE, STEPS, 128), F32),
            pltpu.VMEM((NZ, STEPS, 128), F32),
            pltpu.VMEM((STEPS, 128), F32),
            dma((GROUPS,)), dma((GROUPS,)), dma,
            dma, dma, dma, dma, dma, dma((GROUPS,)), dma, dma, dma, dma((GROUPS,)),
        ],
        compiler_params=pltpu.CompilerParams(
            collective_id=0, has_side_effects=True, vmem_limit_bytes=36 * 1024 * 1024
        ),
        name="sync",
    )(*(pltpu.with_memory_space_constraint(a, pltpu.HBM) for a in (momentum, grads, table)))
    return pl.pallas_call(
        write_kernel,
        out_shape=(
            jax.ShapeDtypeStruct((1, ROWS, COLS), F32),
            jax.ShapeDtypeStruct((ROWS, COLS), BF16),
        ),
        in_specs=[vmem] * 2,
        out_specs=(hbm, hbm),
        scratch_shapes=[dma((GROUPS,)), dma((GROUPS,))],
        compiler_params=pltpu.CompilerParams(vmem_limit_bytes=8 * 1024 * 1024),
        name="write",
    )(*(pltpu.with_memory_space_constraint(a, pltpu.VMEM) for a in (nm, upd)))


def solution(mesh):
    in_specs = (P("replica", None, "tensor"), P("replica", None, None, "tensor"))
    out_specs = (P("replica", None, "tensor"), P(None, "tensor"))
    return jax.shard_map(
        per_device, mesh=mesh, in_specs=in_specs, out_specs=out_specs, check_vma=False
    )
```

```python
import itertools
import math

import jax
import jax.numpy as jnp
import ml_dtypes
import numpy as np
from jax import lax
from jax.experimental import pallas as pl
from jax.experimental.pallas import tpu as pltpu
from jax.sharding import PartitionSpec as P

TILE = 32
BAND = 8
STEPS = 2
BETA = 0.9
CLIP = 1.0
EPS = 1e-06

MESH = pl.DeviceIdType.MESH
F32 = jnp.float32
BF16 = jnp.bfloat16

REP = 32
TEN = 8
NX, NY, NZ, NC = 4, 4, 8, 2
PLANE = NX * NY * NC
BATCHES = ((0, 6, 5, 4), (1, 2, 3))
BEFORE = 3
IDLE = 4
ROWS = 256
COLS = 3456
GCOL = 512
GROUPS = 7
LAST = COLS - (GROUPS - 1) * GCOL
BROW = ROWS // TILE * BAND
BCOL = GCOL // TILE * BAND
QUART = 16
PIECES = GROUPS * (BROW // QUART)


def patterns():
    freq = np.arange(BAND, dtype=np.float64)[:, None]
    place = np.arange(TILE, dtype=np.float64)[None, :]
    weight = np.where(freq == 0, math.sqrt(1.0 / TILE), math.sqrt(2.0 / TILE))
    low = weight * np.cos(math.pi * (2.0 * place + 1.0) * freq / (2.0 * TILE))
    down = np.tile(low.T, (1, GCOL // BAND))
    across = np.tile(low, (1, GCOL // TILE))
    return np.concatenate([down, across], axis=0).astype(np.float32)


def block_diagonal(pattern, times, rows_per, cols_per):
    whole = jnp.concatenate([pattern] * times, axis=0)
    i = lax.broadcasted_iota(jnp.int32, whole.shape, 0) // rows_per
    j = lax.broadcasted_iota(jnp.int32, whole.shape, 1) // cols_per
    return halves(jnp.where(i == j, whole, 0.0))


def encode_tables(pat, wenc, lenc):
    down, across = pat[:TILE], pat[TILE:]
    hi, lo = block_diagonal(down[:, :BCOL], GCOL // TILE, TILE, BAND)
    wenc[:, :BCOL] = hi
    wenc[:, BCOL:] = lo
    hi, lo = block_diagonal(across[:, :ROWS], ROWS // TILE, BAND, TILE)
    lenc[:BROW] = hi
    lenc[BROW:] = lo


def decode_tables(pat, wdec, ldec):
    down, across = pat[:TILE], pat[TILE:]
    hi, lo = block_diagonal(across, GCOL // TILE, BAND, TILE)
    wdec[:BCOL] = hi
    wdec[BCOL:2 * BCOL] = hi
    wdec[2 * BCOL:] = lo
    hi, lo = block_diagonal(down[:, :BROW], ROWS // TILE, TILE, BAND)
    ldec[...] = jnp.concatenate([hi, hi, lo], axis=1)


def halves(a):
    hi = a.astype(BF16)
    return hi, (a - hi.astype(F32)).astype(BF16)


def dot(a, b):
    return jnp.dot(a, b, preferred_element_type=F32)


def decode_group(band, w_dec, l_dec):
    hi, lo = halves(band)
    wide = dot(jnp.concatenate([hi, lo, hi], axis=1), w_dec)
    hi, lo = halves(wide)
    return dot(l_dec, jnp.concatenate([hi, lo, hi], axis=0))


def group_of(plane):
    return plane - lax.div(plane, IDLE + 1)


def plane_of(group):
    return group + group // IDLE


def far(n):
    return sorted(range(n), key=lambda d: -min(d, n - d))


def drain(buf, count, sem):
    part = buf.at[pl.ds(0, count)]
    pltpu.make_async_copy(part, part, sem).wait()


def sync_kernel(
    m_hbm, g_hbm, pat_hbm,
    nm, upd,
    m_v, g_v, pat, wenc, lenc, wdec, ldec, xs, xr, zs, zr, abuf, wide, sq1, sq2, scales,
    g_sem, m_sem, c_sem, p1_send, p1_recv, p2_send, p2_recv, x_send, x_recv, z_send, z_recv, a_send, a_recv,
):
    rep = lax.axis_index("replica")
    ten = lax.axis_index("tensor")
    z, x = lax.div(rep, NX), lax.rem(rep, NX)
    y, c = lax.div(ten, NC), lax.rem(ten, NC)

    zd = [lax.rem(z + d, NZ) for d in range(NZ)]
    xd = [lax.rem(x + d, NX) for d in range(NX)]
    yd = [lax.rem(y + d, NY) * NC for d in range(NY)]
    cd = [c, 1 - c]
    rows = z * NX
    plane_peers = [
        {"replica": rows + xd[dx], "tensor": yd[dy] + cd[dc]}
        for dx, dy, dc in sorted(
            itertools.product(range(NX), range(NY), range(NC)),
            key=lambda d: -(min(d[0], NX - d[0]) + min(d[1], NY - d[1])),
        )
        if dx or dy or dc
    ]
    z_peers = {d: {"replica": zd[d] * NX + x} for d in range(1, NZ)}
    x_peers = {d: {"replica": rows + xd[d]} for d in range(1, NX)}

    def send(src, dst, send_sem, recv_sem, peer):
        pltpu.make_async_remote_copy(
            src_ref=src, dst_ref=dst, send_sem=send_sem, recv_sem=recv_sem, device_id=peer, device_id_type=MESH
        ).start()

    def grad_copy(g, width):
        return pltpu.make_async_copy(
            g_hbm.at[0, :, :, pl.ds(g * GCOL, width)], g_v.at[g, :, :, pl.ds(0, width)], g_sem.at[g]
        )

    def mom_copy(g, width):
        return pltpu.make_async_copy(
            m_hbm.at[0, :, pl.ds(g * GCOL, width)], m_v.at[g, :, pl.ds(0, width)], m_sem.at[g]
        )

    pattern = pltpu.make_async_copy(pat_hbm, pat, c_sem)
    pattern.start()
    widths = [GCOL] * (GROUPS - 1) + [LAST]
    barrier = pltpu.get_barrier_semaphore()

    greeted = [z_peers[d] for d in far(NZ)[:-1]]
    greeted = plane_peers[:8] + greeted + plane_peers[8:]
    for peer in greeted[:12]:
        pl.semaphore_signal(barrier, inc=1, device_id=peer, device_id_type=MESH)
    for g in range(GROUPS):
        grad_copy(g, widths[g]).start()

    for peer in greeted[12:]:
        pl.semaphore_signal(barrier, inc=1, device_id=peer, device_id_type=MESH)


    pattern.wait()
    encode_tables(pat, wenc, lenc)

    m_v[GROUPS - 1, :, LAST:] = jnp.zeros((ROWS, GCOL - LAST), F32)
    g_v[GROUPS - 1, :, :, LAST:] = jnp.zeros((STEPS, ROWS, GCOL - LAST), BF16)

    def squares(g, sums):
        def rows(i, sums):
            at = pl.ds(pl.multiple_of(i * 16, 16), 16)
            x0 = g_v[g, 0, at, :].astype(F32)
            x1 = g_v[g, 1, at, :].astype(F32)
            return sums[0] + x0 * x0, sums[1] + x1 * x1

        return lax.fori_loop(0, ROWS // 16, rows, sums, unroll=16)

    def waited(g, sums):
        grad_copy(g, GCOL).wait()
        mom_copy(g, GCOL).start()
        return squares(g, sums)

    sums = (jnp.zeros((16, GCOL), F32), jnp.zeros((16, GCOL), F32))
    sums = lax.fori_loop(0, GROUPS - 1, waited, sums)
    grad_copy(GROUPS - 1, LAST).wait()
    mom_copy(GROUPS - 1, LAST).start()
    sums = squares(GROUPS - 1, sums)

    def lanes(v):
        v = jnp.sum(v, axis=0, keepdims=True)
        return v[:, :128] + v[:, 128:256] + v[:, 256:384] + v[:, 384:]

    here = (x * NY + y) * NC + c
    sq1[here] = jnp.concatenate([lanes(sums[0]), lanes(sums[1])], axis=0)
    def encode_group(g):
        m_hi, m_lo = halves(m_v[g])
        w = wenc[...]
        cols = [dot(m_hi, w) + dot(m_lo, w)]
        for s in range(STEPS):
            cols.append(dot(g_v[g, s], w))
        wide = jnp.concatenate([v[:, :BCOL] + v[:, BCOL:] for v in cols], axis=1)
        hi, lo = halves(wide)
        first = dot(lenc[...], hi)
        e = first[:BROW] + first[BROW:] + dot(lenc[:BROW], lo)
        for i in range(STEPS + 1):
            xs[:, g, i] = e[:, i * BCOL:(i + 1) * BCOL].reshape(NX, QUART, BCOL)

    def send_quarters(g):
        for d in (2, 1, 3):
            send(xs.at[xd[d], g], xr.at[d - 1, g], x_send, x_recv.at[g], x_peers[d])

    mine_g = group_of(z)

    def turn(k):
        return lax.rem(mine_g + 1 + k, GROUPS)

    def encode_waited(k):
        g = turn(k)

        @pl.when(g < GROUPS - 1)
        def _():
            mom_copy(g, GCOL).wait()

        @pl.when(g == GROUPS - 1)
        def _():
            mom_copy(GROUPS - 1, LAST).wait()

        encode_group(g)
        return g

    def encode_send(k, _):
        send_quarters(encode_waited(k))
        return 0

    ready = encode_waited(0)

    pl.semaphore_wait(barrier, NZ - 1 + PLANE - 1)
    send_quarters(ready)

    for peer in plane_peers:
        send(sq1.at[here], sq1.at[here], p1_send, p1_recv, peer)

    lax.fori_loop(1, GROUPS, encode_send, 0)

    def relay(k, _):
        g = turn(k)
        part = xr.at[:, g]
        pltpu.make_async_copy(part, part, x_recv.at[g]).wait()
        zs[g] = xs[x, g] + xr[0, g] + xr[1, g] + xr[2, g]
        plane = plane_of(g)

        @pl.when(plane != z)
        def _():
            d = lax.rem(plane + NZ - z, NZ)
            send(zs.at[g], zr.at[d - 1], z_send, z_recv, {"replica": plane * NX + x})

        return 0

    lax.fori_loop(0, BEFORE, relay, 0)

    drain(sq1, PLANE - 1, p1_recv)
    sq2[z] = jnp.sum(sq1[...], axis=0)

    for d in far(NZ)[:-1]:
        send(sq2.at[z], sq2.at[z], p2_send, p2_recv, z_peers[d])


    decode_tables(pat, wdec, ldec)

    lax.fori_loop(BEFORE, GROUPS, relay, 0)

    owner = z != IDLE

    @pl.when(owner)
    def _():
        drain(zr, NZ - 1, z_recv)
        zs[mine_g] = zs[mine_g] + jnp.sum(zr[...], axis=0)

    drain(sq2, NZ - 1, p2_recv)
    total = jnp.sum(jnp.sum(sq2[...], axis=0), axis=1, keepdims=True)
    total = jnp.broadcast_to(total, (STEPS, 128))
    count = float(REP * ROWS * TEN * COLS)
    scale = jnp.minimum(1.0, CLIP / jnp.sqrt(total / count + EPS))
    scales[...] = scale

    def momentum_group(g, _):
        sc = scales[...]
        t0, t1 = sc[0:1], sc[1:2]
        own = BETA * (BETA * xs[:, g, 0] + t0 * xs[:, g, 1]) + t1 * xs[:, g, 2]
        low = decode_group(own.reshape(BROW, BCOL), wdec[...], ldec[...])
        state = BETA * m_v[g] + t0[:, 0:1] * g_v[g, 0].astype(F32)
        nm[g] = BETA * state + t1[:, 0:1] * g_v[g, 1].astype(F32) - low
        return 0

    @pl.when(owner)
    def _():
        own = abuf.at[mine_g * NX + x]
        whole = zs[mine_g]
        own[...] = BETA * whole[0] + scale[0:1] * whole[1] + scale[1:2] * whole[2]

        for plane in range(NZ):
            for d in range(1, NX):
                send(own, own, a_send, a_recv.at[mine_g], {"replica": plane * NX + xd[d]})

            @pl.when(plane != z)
            def _():
                send(own, own, a_send, a_recv.at[mine_g], {"replica": plane * NX + x})

    lax.fori_loop(0, GROUPS, momentum_group, 0)

    def await_group(g):
        @pl.when(plane_of(g) == z)
        def _():
            drain(abuf, NX - 1, a_recv.at[g])

        @pl.when(plane_of(g) != z)
        def _():
            drain(abuf, NX, a_recv.at[g])

    for batch in BATCHES:
        for g in batch:
            await_group(g)
        parts = [abuf[g * NX:(g + 1) * NX].reshape(BROW, BCOL) for g in batch]
        hi, lo = halves(jnp.concatenate(parts, axis=0))
        wide[:len(batch) * BROW] = dot(jnp.concatenate([hi, lo, hi], axis=1), wdec[...])
        for i, g in enumerate(batch):
            hi, lo = halves(wide[i * BROW:(i + 1) * BROW])
            upd[g] = dot(ldec[...], jnp.concatenate([hi, lo, hi], axis=0)).astype(BF16)

    drain(sq1, PLANE - 1, p1_send)
    drain(sq2, NZ - 1, p2_send)
    drain(xr, NX - 1, x_send)

    @pl.when(owner)
    def _():
        drain(zs, GROUPS - 1, z_send)
        drain(abuf, PIECES, a_send)
        drain(abuf, REP - 1 - PIECES, a_send)

    @pl.when(jnp.logical_not(owner))
    def _():
        drain(zs, GROUPS, z_send)


def write_kernel(nm, upd, out_m, out_u, m_sem, u_sem):
    copies = []
    for g in range(GROUPS):
        width = GCOL if g < GROUPS - 1 else LAST
        here, there = pl.ds(0, width), pl.ds(g * GCOL, width)
        copies.append(pltpu.make_async_copy(nm.at[g, :, here], out_m.at[0, :, there], m_sem.at[g]))
        copies.append(pltpu.make_async_copy(upd.at[g, :, here], out_u.at[:, there], u_sem.at[g]))
    for copy in copies:
        copy.start()
    for copy in copies:
        copy.wait()


def per_device(momentum, grads):
    table = jnp.asarray(patterns())
    hbm = pl.BlockSpec(memory_space=pl.ANY)
    vmem = pl.BlockSpec(memory_space=pltpu.VMEM)
    dma = pltpu.SemaphoreType.DMA
    nm, upd = pl.pallas_call(
        sync_kernel,
        out_shape=(
            pltpu.VMEM((GROUPS, ROWS, GCOL), F32),
            pltpu.VMEM((GROUPS, ROWS, GCOL), BF16),
        ),
        in_specs=[hbm] * 3,
        out_specs=(vmem,) * 2,
        scratch_shapes=[
            pltpu.VMEM((GROUPS, ROWS, GCOL), F32),
            pltpu.VMEM((GROUPS, STEPS, ROWS, GCOL), BF16),
            pltpu.VMEM((TILE + BAND, GCOL), F32),
            pltpu.VMEM((GCOL, 2 * BCOL), BF16),
            pltpu.VMEM((2 * BROW, ROWS), BF16),
            pltpu.VMEM((3 * BCOL, GCOL), BF16),
            pltpu.VMEM((ROWS, 3 * BROW), BF16),
            pltpu.VMEM((NX, GROUPS, STEPS + 1, QUART, BCOL), F32),
            pltpu.VMEM((NX - 1, GROUPS, STEPS + 1, QUART, BCOL), F32),
            pltpu.VMEM((GROUPS, STEPS + 1, QUART, BCOL), F32),
            pltpu.VMEM((NZ - 1, STEPS + 1, QUART, BCOL), F32),
            pltpu.VMEM((PIECES, QUART, BCOL), F32),
            pltpu.VMEM((GROUPS * BROW, GCOL), F32),
            pltpu.VMEM((PLANE, STEPS, 128), F32),
            pltpu.VMEM((NZ, STEPS, 128), F32),
            pltpu.VMEM((STEPS, 128), F32),
            dma((GROUPS,)), dma((GROUPS,)), dma,
            dma, dma, dma, dma, dma, dma((GROUPS,)), dma, dma, dma, dma((GROUPS,)),
        ],
        compiler_params=pltpu.CompilerParams(
            collective_id=0, has_side_effects=True, vmem_limit_bytes=36 * 1024 * 1024
        ),
        name="sync",
    )(*(pltpu.with_memory_space_constraint(a, pltpu.HBM) for a in (momentum, grads, table)))
    return pl.pallas_call(
        write_kernel,
        out_shape=(
            jax.ShapeDtypeStruct((1, ROWS, COLS), F32),
            jax.ShapeDtypeStruct((ROWS, COLS), BF16),
        ),
        in_specs=[vmem] * 2,
        out_specs=(hbm, hbm),
        scratch_shapes=[dma((GROUPS,)), dma((GROUPS,))],
        compiler_params=pltpu.CompilerParams(vmem_limit_bytes=8 * 1024 * 1024),
        name="write",
    )(*(pltpu.with_memory_space_constraint(a, pltpu.VMEM) for a in (nm, upd)))


def solution(mesh):
    in_specs = (P("replica", None, "tensor"), P("replica", None, None, "tensor"))
    out_specs = (P("replica", None, "tensor"), P(None, "tensor"))
    return jax.shard_map(
        per_device, mesh=mesh, in_specs=in_specs, out_specs=out_specs, check_vma=False
    )
```

```python
import itertools
import math

import jax
import jax.numpy as jnp
import ml_dtypes
import numpy as np
from jax import lax
from jax.experimental import pallas as pl
from jax.experimental.pallas import tpu as pltpu
from jax.sharding import PartitionSpec as P

TILE = 32
BAND = 8
STEPS = 2
BETA = 0.9
CLIP = 1.0
EPS = 1e-06

MESH = pl.DeviceIdType.MESH
F32 = jnp.float32
BF16 = jnp.bfloat16

REP = 32
TEN = 8
NX, NY, NZ, NC = 4, 4, 8, 2
PLANE = NX * NY * NC
BATCHES = ((0, 6, 5, 4), (1, 2, 3))
BEFORE = 5
IDLE = 4
ROWS = 256
COLS = 3456
GCOL = 512
GROUPS = 7
LAST = COLS - (GROUPS - 1) * GCOL
BROW = ROWS // TILE * BAND
BCOL = GCOL // TILE * BAND
QUART = 16
PIECES = GROUPS * (BROW // QUART)


def patterns():
    freq = np.arange(BAND, dtype=np.float64)[:, None]
    place = np.arange(TILE, dtype=np.float64)[None, :]
    weight = np.where(freq == 0, math.sqrt(1.0 / TILE), math.sqrt(2.0 / TILE))
    low = weight * np.cos(math.pi * (2.0 * place + 1.0) * freq / (2.0 * TILE))
    down = np.tile(low.T, (1, GCOL // BAND))
    across = np.tile(low, (1, GCOL // TILE))
    return np.concatenate([down, across], axis=0).astype(np.float32)


def block_diagonal(pattern, times, rows_per, cols_per):
    whole = jnp.concatenate([pattern] * times, axis=0)
    i = lax.broadcasted_iota(jnp.int32, whole.shape, 0) // rows_per
    j = lax.broadcasted_iota(jnp.int32, whole.shape, 1) // cols_per
    return halves(jnp.where(i == j, whole, 0.0))


def encode_tables(pat, wenc, lenc):
    down, across = pat[:TILE], pat[TILE:]
    hi, lo = block_diagonal(down[:, :BCOL], GCOL // TILE, TILE, BAND)
    wenc[:, :BCOL] = hi
    wenc[:, BCOL:] = lo
    hi, lo = block_diagonal(across[:, :ROWS], ROWS // TILE, BAND, TILE)
    lenc[:BROW] = hi
    lenc[BROW:] = lo


def decode_tables(pat, wdec, ldec):
    down, across = pat[:TILE], pat[TILE:]
    hi, lo = block_diagonal(across, GCOL // TILE, BAND, TILE)
    wdec[:BCOL] = hi
    wdec[BCOL:2 * BCOL] = hi
    wdec[2 * BCOL:] = lo
    hi, lo = block_diagonal(down[:, :BROW], ROWS // TILE, TILE, BAND)
    ldec[...] = jnp.concatenate([hi, hi, lo], axis=1)


def halves(a):
    hi = a.astype(BF16)
    return hi, (a - hi.astype(F32)).astype(BF16)


def dot(a, b):
    return jnp.dot(a, b, preferred_element_type=F32)


def decode_group(band, w_dec, l_dec):
    hi, lo = halves(band)
    wide = dot(jnp.concatenate([hi, lo, hi], axis=1), w_dec)
    hi, lo = halves(wide)
    return dot(l_dec, jnp.concatenate([hi, lo, hi], axis=0))


def group_of(plane):
    return plane - lax.div(plane, IDLE + 1)


def plane_of(group):
    return group + group // IDLE


def far(n):
    return sorted(range(n), key=lambda d: -min(d, n - d))


def drain(buf, count, sem):
    part = buf.at[pl.ds(0, count)]
    pltpu.make_async_copy(part, part, sem).wait()


def sync_kernel(
    m_hbm, g_hbm, pat_hbm,
    nm, upd,
    m_v, g_v, pat, wenc, lenc, wdec, ldec, xs, xr, zs, zr, abuf, wide, sq1, sq2, scales,
    g_sem, m_sem, c_sem, p1_send, p1_recv, p2_send, p2_recv, x_send, x_recv, z_send, z_recv, a_send, a_recv,
):
    rep = lax.axis_index("replica")
    ten = lax.axis_index("tensor")
    z, x = lax.div(rep, NX), lax.rem(rep, NX)
    y, c = lax.div(ten, NC), lax.rem(ten, NC)

    zd = [lax.rem(z + d, NZ) for d in range(NZ)]
    xd = [lax.rem(x + d, NX) for d in range(NX)]
    yd = [lax.rem(y + d, NY) * NC for d in range(NY)]
    cd = [c, 1 - c]
    rows = z * NX
    plane_peers = [
        {"replica": rows + xd[dx], "tensor": yd[dy] + cd[dc]}
        for dx, dy, dc in sorted(
            itertools.product(range(NX), range(NY), range(NC)),
            key=lambda d: -(min(d[0], NX - d[0]) + min(d[1], NY - d[1])),
        )
        if dx or dy or dc
    ]
    z_peers = {d: {"replica": zd[d] * NX + x} for d in range(1, NZ)}
    x_peers = {d: {"replica": rows + xd[d]} for d in range(1, NX)}

    def send(src, dst, send_sem, recv_sem, peer):
        pltpu.make_async_remote_copy(
            src_ref=src, dst_ref=dst, send_sem=send_sem, recv_sem=recv_sem, device_id=peer, device_id_type=MESH
        ).start()

    def grad_copy(g, width):
        return pltpu.make_async_copy(
            g_hbm.at[0, :, :, pl.ds(g * GCOL, width)], g_v.at[g, :, :, pl.ds(0, width)], g_sem.at[g]
        )

    def mom_copy(g, width):
        return pltpu.make_async_copy(
            m_hbm.at[0, :, pl.ds(g * GCOL, width)], m_v.at[g, :, pl.ds(0, width)], m_sem.at[g]
        )

    pattern = pltpu.make_async_copy(pat_hbm, pat, c_sem)
    pattern.start()
    widths = [GCOL] * (GROUPS - 1) + [LAST]
    barrier = pltpu.get_barrier_semaphore()

    greeted = [z_peers[d] for d in far(NZ)[:-1]]
    greeted = plane_peers[:8] + greeted + plane_peers[8:]
    for peer in greeted[:12]:
        pl.semaphore_signal(barrier, inc=1, device_id=peer, device_id_type=MESH)
    for g in range(GROUPS):
        grad_copy(g, widths[g]).start()

    for peer in greeted[12:]:
        pl.semaphore_signal(barrier, inc=1, device_id=peer, device_id_type=MESH)


    pattern.wait()
    encode_tables(pat, wenc, lenc)

    m_v[GROUPS - 1, :, LAST:] = jnp.zeros((ROWS, GCOL - LAST), F32)
    g_v[GROUPS - 1, :, :, LAST:] = jnp.zeros((STEPS, ROWS, GCOL - LAST), BF16)

    def squares(g, sums):
        def rows(i, sums):
            at = pl.ds(pl.multiple_of(i * 16, 16), 16)
            x0 = g_v[g, 0, at, :].astype(F32)
            x1 = g_v[g, 1, at, :].astype(F32)
            return sums[0] + x0 * x0, sums[1] + x1 * x1

        return lax.fori_loop(0, ROWS // 16, rows, sums, unroll=4)

    def waited(g, sums):
        grad_copy(g, GCOL).wait()
        mom_copy(g, GCOL).start()
        return squares(g, sums)

    sums = (jnp.zeros((16, GCOL), F32), jnp.zeros((16, GCOL), F32))
    sums = lax.fori_loop(0, GROUPS - 1, waited, sums)
    grad_copy(GROUPS - 1, LAST).wait()
    mom_copy(GROUPS - 1, LAST).start()
    sums = squares(GROUPS - 1, sums)

    def lanes(v):
        v = jnp.sum(v, axis=0, keepdims=True)
        return v[:, :128] + v[:, 128:256] + v[:, 256:384] + v[:, 384:]

    here = (x * NY + y) * NC + c
    sq1[here] = jnp.concatenate([lanes(sums[0]), lanes(sums[1])], axis=0)
    def encode_group(g):
        m_hi, m_lo = halves(m_v[g])
        w = wenc[...]
        cols = [dot(m_hi, w) + dot(m_lo, w)]
        for s in range(STEPS):
            cols.append(dot(g_v[g, s], w))
        wide = jnp.concatenate([v[:, :BCOL] + v[:, BCOL:] for v in cols], axis=1)
        hi, lo = halves(wide)
        first = dot(lenc[...], hi)
        e = first[:BROW] + first[BROW:] + dot(lenc[:BROW], lo)
        for i in range(STEPS + 1):
            xs[:, g, i] = e[:, i * BCOL:(i + 1) * BCOL].reshape(NX, QUART, BCOL)

    def send_quarters(g):
        for d in (2, 1, 3):
            send(xs.at[xd[d], g], xr.at[d - 1, g], x_send, x_recv.at[g], x_peers[d])

    mine_g = group_of(z)

    def turn(k):
        return lax.rem(mine_g + 1 + k, GROUPS)

    def encode_waited(k):
        g = turn(k)

        @pl.when(g < GROUPS - 1)
        def _():
            mom_copy(g, GCOL).wait()

        @pl.when(g == GROUPS - 1)
        def _():
            mom_copy(GROUPS - 1, LAST).wait()

        encode_group(g)
        return g

    def encode_send(k, _):
        send_quarters(encode_waited(k))
        return 0

    ready = encode_waited(0)

    pl.semaphore_wait(barrier, NZ - 1 + PLANE - 1)
    send_quarters(ready)

    for peer in plane_peers:
        send(sq1.at[here], sq1.at[here], p1_send, p1_recv, peer)

    lax.fori_loop(1, GROUPS, encode_send, 0)

    def relay(k, _):
        g = turn(k)
        part = xr.at[:, g]
        pltpu.make_async_copy(part, part, x_recv.at[g]).wait()
        zs[g] = xs[x, g] + xr[0, g] + xr[1, g] + xr[2, g]
        plane = plane_of(g)

        @pl.when(plane != z)
        def _():
            d = lax.rem(plane + NZ - z, NZ)
            send(zs.at[g], zr.at[d - 1], z_send, z_recv, {"replica": plane * NX + x})

        return 0

    lax.fori_loop(0, BEFORE, relay, 0)

    drain(sq1, PLANE - 1, p1_recv)
    sq2[z] = jnp.sum(sq1[...], axis=0)

    for d in far(NZ)[:-1]:
        send(sq2.at[z], sq2.at[z], p2_send, p2_recv, z_peers[d])


    decode_tables(pat, wdec, ldec)

    lax.fori_loop(BEFORE, GROUPS, relay, 0)

    drain(sq2, NZ - 1, p2_recv)
    total = jnp.sum(jnp.sum(sq2[...], axis=0), axis=1, keepdims=True)
    total = jnp.broadcast_to(total, (STEPS, 128))
    count = float(REP * ROWS * TEN * COLS)
    scale = jnp.minimum(1.0, CLIP / jnp.sqrt(total / count + EPS))
    scales[...] = scale

    def momentum_group(g, _):
        sc = scales[...]
        t0, t1 = sc[0:1], sc[1:2]
        own = BETA * (BETA * xs[:, g, 0] + t0 * xs[:, g, 1]) + t1 * xs[:, g, 2]
        low = decode_group(own.reshape(BROW, BCOL), wdec[...], ldec[...])
        state = BETA * m_v[g] + t0[:, 0:1] * g_v[g, 0].astype(F32)
        nm[g] = BETA * state + t1[:, 0:1] * g_v[g, 1].astype(F32) - low
        return 0

    owner = z != IDLE

    @pl.when(owner)
    def _():
        drain(zr, NZ - 1, z_recv)
        own = abuf.at[mine_g * NX + x]
        whole = zs[mine_g] + jnp.sum(zr[...], axis=0)
        own[...] = BETA * whole[0] + scale[0:1] * whole[1] + scale[1:2] * whole[2]

        for plane in range(NZ):
            for d in range(1, NX):
                send(own, own, a_send, a_recv.at[mine_g], {"replica": plane * NX + xd[d]})

            @pl.when(plane != z)
            def _():
                send(own, own, a_send, a_recv.at[mine_g], {"replica": plane * NX + x})

    lax.fori_loop(0, GROUPS, momentum_group, 0)

    def await_group(g):
        @pl.when(plane_of(g) == z)
        def _():
            drain(abuf, NX - 1, a_recv.at[g])

        @pl.when(plane_of(g) != z)
        def _():
            drain(abuf, NX, a_recv.at[g])

    for batch in BATCHES:
        for g in batch:
            await_group(g)
        parts = [abuf[g * NX:(g + 1) * NX].reshape(BROW, BCOL) for g in batch]
        hi, lo = halves(jnp.concatenate(parts, axis=0))
        wide[:len(batch) * BROW] = dot(jnp.concatenate([hi, lo, hi], axis=1), wdec[...])
        for i, g in enumerate(batch):
            hi, lo = halves(wide[i * BROW:(i + 1) * BROW])
            upd[g] = dot(ldec[...], jnp.concatenate([hi, lo, hi], axis=0)).astype(BF16)

    drain(sq1, PLANE - 1, p1_send)
    drain(sq2, NZ - 1, p2_send)
    drain(xr, NX - 1, x_send)

    @pl.when(owner)
    def _():
        drain(zs, GROUPS - 1, z_send)
        drain(abuf, PIECES, a_send)
        drain(abuf, REP - 1 - PIECES, a_send)

    @pl.when(jnp.logical_not(owner))
    def _():
        drain(zs, GROUPS, z_send)


def write_kernel(nm, upd, out_m, out_u, m_sem, u_sem):
    copies = []
    for g in range(GROUPS):
        width = GCOL if g < GROUPS - 1 else LAST
        here, there = pl.ds(0, width), pl.ds(g * GCOL, width)
        copies.append(pltpu.make_async_copy(nm.at[g, :, here], out_m.at[0, :, there], m_sem.at[g]))
        copies.append(pltpu.make_async_copy(upd.at[g, :, here], out_u.at[:, there], u_sem.at[g]))
    for copy in copies:
        copy.start()
    for copy in copies:
        copy.wait()


def per_device(momentum, grads):
    table = jnp.asarray(patterns())
    hbm = pl.BlockSpec(memory_space=pl.ANY)
    vmem = pl.BlockSpec(memory_space=pltpu.VMEM)
    dma = pltpu.SemaphoreType.DMA
    nm, upd = pl.pallas_call(
        sync_kernel,
        out_shape=(
            pltpu.VMEM((GROUPS, ROWS, GCOL), F32),
            pltpu.VMEM((GROUPS, ROWS, GCOL), BF16),
        ),
        in_specs=[hbm] * 3,
        out_specs=(vmem,) * 2,
        scratch_shapes=[
            pltpu.VMEM((GROUPS, ROWS, GCOL), F32),
            pltpu.VMEM((GROUPS, STEPS, ROWS, GCOL), BF16),
            pltpu.VMEM((TILE + BAND, GCOL), F32),
            pltpu.VMEM((GCOL, 2 * BCOL), BF16),
            pltpu.VMEM((2 * BROW, ROWS), BF16),
            pltpu.VMEM((3 * BCOL, GCOL), BF16),
            pltpu.VMEM((ROWS, 3 * BROW), BF16),
            pltpu.VMEM((NX, GROUPS, STEPS + 1, QUART, BCOL), F32),
            pltpu.VMEM((NX - 1, GROUPS, STEPS + 1, QUART, BCOL), F32),
            pltpu.VMEM((GROUPS, STEPS + 1, QUART, BCOL), F32),
            pltpu.VMEM((NZ - 1, STEPS + 1, QUART, BCOL), F32),
            pltpu.VMEM((PIECES, QUART, BCOL), F32),
            pltpu.VMEM((GROUPS * BROW, GCOL), F32),
            pltpu.VMEM((PLANE, STEPS, 128), F32),
            pltpu.VMEM((NZ, STEPS, 128), F32),
            pltpu.VMEM((STEPS, 128), F32),
            dma((GROUPS,)), dma((GROUPS,)), dma,
            dma, dma, dma, dma, dma, dma((GROUPS,)), dma, dma, dma, dma((GROUPS,)),
        ],
        compiler_params=pltpu.CompilerParams(
            collective_id=0, has_side_effects=True, vmem_limit_bytes=36 * 1024 * 1024
        ),
        name="sync",
    )(*(pltpu.with_memory_space_constraint(a, pltpu.HBM) for a in (momentum, grads, table)))
    return pl.pallas_call(
        write_kernel,
        out_shape=(
            jax.ShapeDtypeStruct((1, ROWS, COLS), F32),
            jax.ShapeDtypeStruct((ROWS, COLS), BF16),
        ),
        in_specs=[vmem] * 2,
        out_specs=(hbm, hbm),
        scratch_shapes=[dma((GROUPS,)), dma((GROUPS,))],
        compiler_params=pltpu.CompilerParams(vmem_limit_bytes=8 * 1024 * 1024),
        name="write",
    )(*(pltpu.with_memory_space_constraint(a, pltpu.VMEM) for a in (nm, upd)))


def solution(mesh):
    in_specs = (P("replica", None, "tensor"), P("replica", None, None, "tensor"))
    out_specs = (P("replica", None, "tensor"), P(None, "tensor"))
    return jax.shard_map(
        per_device, mesh=mesh, in_specs=in_specs, out_specs=out_specs, check_vma=False
    )
```
